256 devices in a mesh: grp: 8 (over x, core), seq: 32 (over y, z).
Axes of the slice: x: 4, y: 4, z: 8, core: 2. Of those that a mesh axis runs over, the one named last changes fastest.
Arguments:
- features: bfloat16 [65536, 2048], P(('grp', 'seq')), may hold values from -6 to 6
- gate_input: bfloat16 [65536, 2048], P(('grp', 'seq')), may hold values from -6 to 6
- b_forward: bfloat16 [65536, 128], P(('grp', 'seq')), may hold values from -6 to 6
- c_forward: bfloat16 [65536, 128], P(('grp', 'seq')), may hold values from -6 to 6
- b_backward: bfloat16 [65536, 128], P(('grp', 'seq')), may hold values from -6 to 6
- c_backward: bfloat16 [65536, 128], P(('grp', 'seq')), may hold values from -6 to 6
- rate_forward: float32 [32, 65536], P(None, ('grp', 'seq')), may hold values from 3.0517578e-07 to 0.8, as said below
- rate_backward: float32 [32, 65536], P(None, ('grp', 'seq')), may hold values from 3.0517578e-07 to 0.8, as said below
- norm_gain: float32 [2048], replicated, may hold values from 0.5 to 1.5
- out_weight: bfloat16 [2048, 1024], replicated, may hold values from -0.125 to 0.125
Outputs:
- mixed: bfloat16 [65536, 1024], P(('grp', 'seq'))
The draws below stay inside these ranges and needn't reach their ends.
Inputs may be any that keep to these rules, and one draw needn't show every extreme that they name: `rate_forward`: positive decay rates; one token keeps exp(-rate) of a head's state. `rate_backward`: positive decay rates; one token keeps exp(-rate) of a head's state.
All inputs are finite; a program needn't handle non-finite values.
Results may differ from the reference program's by a relative error of at most 0.019.
Values may be sent and summed in bfloat16 or wider, within the bound.
No kernel may reach another device: no remote copies, remote signals or barrier semaphores. Data moves between devices by JAX's collectives and lax.ppermute only.
A program may use at most 64 MiB of HBM per device.

```python
import math
import jax
import jax.numpy as jnp
from jax import lax

D = 1024
H = 32
P_SIZE = 64
N = 128
Q = 256
TOK_DEV = 256
E = 2048
SEQ = 65536


def rate_table(key, fast_share):
    keys = jax.random.split(key, 14)
    token_position = jnp.arange(SEQ)
    head_number = jnp.arange(H)[:, None]
    span_count = SEQ // Q
    fast_heads = jax.random.uniform(keys[0], (H, 1)) < fast_share
    slow_rate = jnp.exp(jax.random.uniform(keys[1], (H, 1), minval=math.log(0.1), maxval=math.log(0.6))) / SEQ
    quick_rate = jnp.exp(jax.random.uniform(keys[2], (H, 1), minval=math.log(1.0 / 50.0), maxval=math.log(1.0 / 30.0)))
    baseline_rate = jnp.where(fast_heads, quick_rate, slow_rate)
    coarse_noise = jnp.exp(jax.random.uniform(keys[3], (H, SEQ), minval=-0.693, maxval=0.693))
    phase = jax.random.uniform(keys[4], (H, 1))
    token_region = jnp.exp(0.7 * jnp.sin(2.0 * math.pi * (3.0 * token_position.astype(jnp.float32)[None, :] / SEQ + phase)))
    marked_places = jax.random.randint(keys[5], (H, 1), 0, SEQ)
    dropped_values = -jnp.log(jax.random.uniform(keys[6], (H, 1), minval=0.55, maxval=0.8))
    sudden_surge = jnp.where(token_position[None, :] == marked_places, dropped_values, 0.0)
    deep_span = jax.random.randint(keys[7], (H, 1), span_count // 4, 3 * span_count // 4 + 1)
    deep_offset = jax.random.randint(keys[8], (H, 1), 0, Q - 3)
    deep_start = deep_span * Q + deep_offset
    strong_head = jax.random.randint(keys[9], (), 0, H)
    deep_total = jnp.where(head_number == strong_head, jax.random.uniform(keys[10], (H, 1), minval=2.6, maxval=3.0), jax.random.uniform(keys[11], (H, 1), minval=1.05, maxval=1.3))
    inside_deep = (token_position[None, :] >= deep_start) & (token_position[None, :] < deep_start + 4)
    deep_surge = jnp.where(inside_deep, deep_total / 4.0, 0.0)
    rates = jnp.minimum(baseline_rate * coarse_noise * token_region + sudden_surge + deep_surge, 0.8)
    hot_pick = jax.random.randint(keys[12], (2,), 0, H * span_count)
    hot_head = hot_pick[0] % H
    hot_span = hot_pick[1] % span_count
    inside_hot = (head_number == hot_head) & (token_position[None, :] // Q == hot_span)
    hot_values = jax.random.uniform(keys[13], (H, SEQ), minval=0.5, maxval=0.8)
    rates = jnp.where(inside_hot, hot_values, rates)
    return rates.astype(jnp.float32)


def draw_rate_forward(key, part):
    key = jax.random.fold_in(key, 11)
    return rate_table(key, 0.5)


def draw_rate_backward(key, part):
    key = jax.random.fold_in(key, 23)
    return rate_table(key, 0.5)


def steps_of(own_key, shape, cuts, low, largest):
    factor_of, own = 1.0, jax.random.fold_in(own_key, 6)
    for dim, shards_of in cuts:
        steps = jnp.exp(jax.random.uniform(jax.random.fold_in(own, dim), (shards_of,), jnp.float32, low / len(cuts), largest / len(cuts)))
        factor_of = factor_of * jnp.repeat(steps, shape[dim] // shards_of).reshape([-1 if axis == dim else 1 for axis in range(len(shape))])
    return factor_of


def bell_draw(own_key, dims, scale, most, shards=(), dtype=jnp.bfloat16):
    result = jax.random.normal(own_key, dims, jnp.float32) * scale
    if len(shards) > 0:
        result = steps_of(own_key, dims, shards, -0.22, 0.18) * result
    return jnp.clip(result, min=-most, max=most).astype(dtype)


def setup_inputs(seed: int = 0) -> dict:
    arg_keys = jax.random.split(jax.random.key(seed), 11)
    return {
        "features": bell_draw(arg_keys[0], (SEQ, E), 1.0, 6.0, ((0, 256),)),
        "gate_input": bell_draw(arg_keys[1], (SEQ, E), 1.0, 6.0, ((0, 256),)),
        "b_forward": bell_draw(arg_keys[2], (SEQ, N), 1.0, 6.0, ((0, 256),)),
        "c_forward": bell_draw(arg_keys[3], (SEQ, N), 1.0, 6.0, ((0, 256),)),
        "b_backward": bell_draw(arg_keys[4], (SEQ, N), 1.0, 6.0, ((0, 256),)),
        "c_backward": bell_draw(arg_keys[5], (SEQ, N), 1.0, 6.0, ((0, 256),)),
        "rate_forward": draw_rate_forward(jax.random.fold_in(arg_keys[10], 71), 0),
        "rate_backward": draw_rate_backward(jax.random.fold_in(arg_keys[10], 71), 0),
        "norm_gain": jnp.clip(1.0 + 0.1 * jax.random.normal(arg_keys[8], (E,), jnp.float32), 0.5, 1.5),
        "out_weight": bell_draw(arg_keys[9], (E, D), E ** -0.5, 0.125),
    }


def scaled_inputs(features, decay_rate):
    step_size = jnp.sqrt(-jnp.expm1(-2.0 * decay_rate))
    values = features.reshape(SEQ, H, P_SIZE).astype(jnp.float32)
    return (values * step_size.T[:, :, None]).astype(jnp.bfloat16)

def one_direction(inputs, b_map, c_map, decay_rate):
    count = SEQ // Q
    x_blocks = inputs.reshape(count, Q, H, P_SIZE)
    b_blocks = b_map.reshape(count, Q, N)
    c_blocks = c_map.reshape(count, Q, N)
    r_blocks = decay_rate.reshape(H, count, Q).transpose(1, 0, 2)
    below_diag = jnp.arange(Q)[:, None] >= jnp.arange(Q)[None, :]

    def advance(carried, blocks):
        x_part, b_part, c_part, r_part = blocks
        cumulative = jnp.cumsum(r_part, axis=1)
        scores = jnp.dot(c_part, b_part.T, preferred_element_type=jnp.float32)
        log_gap = jnp.where(below_diag[None], cumulative[:, :, None] - cumulative[:, None, :], 0.0)
        weights = jnp.where(below_diag[None], scores[None] * jnp.exp(-log_gap), 0.0).astype(jnp.bfloat16)
        weights = lax.optimization_barrier(weights).astype(jnp.float32)
        inside = jnp.einsum('hts,shp->thp', weights, x_part.astype(jnp.float32))
        entry_state = lax.optimization_barrier(carried.astype(jnp.bfloat16)).astype(jnp.float32)
        from_state = jnp.einsum('tn,hpn->thp', c_part.astype(jnp.float32), entry_state)
        from_state = from_state * jnp.exp(-cumulative).T[:, :, None]
        to_end = jnp.exp(cumulative - cumulative[:, -1:])
        decayed = (x_part.astype(jnp.float32) * to_end.T[:, :, None]).astype(jnp.bfloat16)
        decayed = lax.optimization_barrier(decayed).astype(jnp.float32)
        own_state = jnp.einsum('shp,sn->hpn', decayed, b_part.astype(jnp.float32))
        carried = jnp.exp(-cumulative[:, -1])[:, None, None] * carried + own_state
        return (carried, inside + from_state)
    start_state = jnp.zeros((H, P_SIZE, N), jnp.float32)
    _, results = lax.scan(advance, start_state, (x_blocks, b_blocks, c_blocks, r_blocks))
    return results.reshape(SEQ, H, P_SIZE)

def reference(features, gate_input, b_forward, c_forward, b_backward, c_backward, rate_forward, rate_backward, norm_gain, out_weight):
    forward = one_direction(scaled_inputs(features, rate_forward), b_forward, c_forward, rate_forward)
    flipped_rate = jnp.flip(rate_backward, axis=1)
    backward = one_direction(scaled_inputs(jnp.flip(features, 0), flipped_rate), jnp.flip(b_backward, 0), jnp.flip(c_backward, 0), flipped_rate)
    combined = (forward + jnp.flip(backward, 0)).reshape(SEQ, E)

    def finish(pieces):
        block_rows, gate_rows = pieces
        gated_rows = block_rows * jax.nn.silu(gate_rows.astype(jnp.float32))
        inverse_rms = lax.rsqrt(lax.optimization_barrier(jnp.mean(gated_rows * gated_rows, axis=1, keepdims=True)) + 1e-05)
        normed = (gated_rows * inverse_rms * norm_gain).astype(jnp.bfloat16)
        return jnp.dot(normed, out_weight, preferred_element_type=jnp.float32).astype(jnp.bfloat16)
    mixed = lax.map(finish, (combined.reshape(SEQ // TOK_DEV, TOK_DEV, E), gate_input.reshape(SEQ // TOK_DEV, TOK_DEV, E)))
    return mixed.reshape(SEQ, D)
```

```python
import functools
import jax
import jax.numpy as jnp
from jax import lax
from jax.experimental import pallas as pl
from jax.experimental.pallas import tpu as pltpu
from jax.sharding import PartitionSpec as P

Q = 256
H = 32
HEAD = 64
N = 128
E = 2048
D = 1024
BLK = 256
STEPS = E // BLK
HPB = BLK // HEAD
ROWS = N + 16
LOG2E = 1.4426950408889634
F32 = jnp.float32
BF16 = jnp.bfloat16


def lane_sums(r):
    width = r.shape[1]
    lane = lax.broadcasted_iota(jnp.int32, r.shape, 1)
    shift = 1
    while shift < width:
        r = r + jnp.where(lane >= shift, pltpu.roll(r, shift, 1), 0.0)
        shift *= 2
    return r


def lane_sums_back(r):
    width = r.shape[1]
    lane = lax.broadcasted_iota(jnp.int32, r.shape, 1)
    shift = 1
    while shift < width:
        r = r + jnp.where(lane < width - shift, pltpu.roll(r, width - shift, 1), 0.0)
        shift *= 2
    return r


def step_of(r):
    y = 2.0 * r
    s = jnp.full_like(y, 1.0)
    for k in range(9, 1, -1):
        s = 1.0 - y * (1.0 / k) * s
    return jnp.sqrt(jnp.where(y < 0.5, y * s, 1.0 - jnp.exp(-y)))


def two_parts(a):
    high = a.astype(BF16).astype(F32)
    return high, a - high


def head_select(block, rows, width, first, pairs):
    row = lax.broadcasted_iota(jnp.int32, (rows, width), 0)
    column = lax.broadcasted_iota(jnp.int32, (rows, width), 1)
    head = block * HPB + column // HEAD
    hit = (row % H == head) & (row >= first) & (row < first + pairs * H)
    return jnp.where(hit, 1.0, 0.0).astype(BF16)


def dot(a, b):
    return jnp.dot(a, b, preferred_element_type=F32)


def state_kernel(x_ref, rf_ref, rb_ref, bf_ref, bb_ref, out_ref, scale_ref, bt_ref, keep_ref):
    j = pl.program_id(0)

    @pl.when(j == 0)
    def _():
        parts = []
        for d, (r_ref, sums) in enumerate(((rf_ref, lane_sums), (rb_ref, lane_sums_back))):
            r = r_ref[...]
            c = sums(r)
            total = c[:, Q - 1 : Q] if d == 0 else c[:, 0:1]
            parts += two_parts(step_of(r) * jnp.exp(c - total))
            keep_ref[d] = jnp.broadcast_to(jnp.exp(-total), (H, 128))
        scale_ref[...] = jnp.concatenate(parts, axis=0).T.astype(BF16)
        bt_ref[0] = bf_ref[...].astype(F32).T.astype(BF16)
        bt_ref[1] = bb_ref[...].astype(F32).T.astype(BF16)

    x = x_ref[...].astype(F32)
    for d in range(2):
        factor = dot(scale_ref[...], head_select(j, 4 * H, BLK, 2 * H * d, 2))
        v = (x * factor).astype(BF16)
        s = dot(bt_ref[d], v).astype(BF16)
        head = lax.broadcasted_iota(jnp.int32, (H, BLK), 0)
        column = lax.broadcasted_iota(jnp.int32, (H, BLK), 1)
        keep = jnp.concatenate([keep_ref[d]] * (BLK // 128), axis=1)
        keep = jnp.sum(
            jnp.where(head == j * HPB + column // HEAD, keep, 0.0), axis=0, keepdims=True
        )
        high, rest = two_parts(keep)
        middle, low = two_parts(rest)
        row = lax.broadcasted_iota(jnp.int32, (16, BLK), 0)
        tail = jnp.where(row == 0, high, jnp.where(row == 1, middle, jnp.where(row == 2, low, 0.0)))
        tail = tail.astype(BF16)
        for k in range(BLK // 128):
            out_ref[d, k, 0:N, :] = s[:, 128 * k : 128 * (k + 1)]
            out_ref[d, k, N:ROWS, :] = tail[:, 128 * k : 128 * (k + 1)]


def state_call(x, rate_f, rate_b, b_f, b_b):
    whole = lambda shape: pl.BlockSpec(shape, lambda j: (0,) * len(shape))
    return pl.pallas_call(
        state_kernel,
        grid=(STEPS,),
        in_specs=[
            pl.BlockSpec((Q, BLK), lambda j: (0, j)),
            whole((H, Q)),
            whole((H, Q)),
            whole((Q, N)),
            whole((Q, N)),
        ],
        out_specs=pl.BlockSpec((2, BLK // 128, ROWS, 128), lambda j: (0, j, 0, 0)),
        out_shape=jax.ShapeDtypeStruct((2, E // 128, ROWS, 128), BF16),
        scratch_shapes=[
            pltpu.VMEM((Q, 4 * H), BF16),
            pltpu.VMEM((2, N, Q), BF16),
            pltpu.VMEM((2, H, 128), F32),
        ],
        name="span_states",
    )(x, rate_f, rate_b, b_f, b_b)


def inside_kernel(
    x_ref, gate_ref, rf_ref, rb_ref, bf_ref, cf_ref, bb_ref, cb_ref,
    out_ref, silu_ref, score_ref, rows_ref, cols_ref,
):
    j = pl.program_id(0)
    t = lax.broadcasted_iota(jnp.int32, (Q, Q), 0)
    s = lax.broadcasted_iota(jnp.int32, (Q, Q), 1)

    @pl.when(j == 0)
    def _():
        contract = (((1,), (1,)), ((), ()))
        forward = lax.dot_general(cf_ref[...], bf_ref[...], contract, preferred_element_type=F32)
        backward = lax.dot_general(cb_ref[...], bb_ref[...], contract, preferred_element_type=F32)
        score_ref[...] = jnp.where(s <= t, forward, backward)
        own = jnp.sum(jnp.where(s == t, backward, 0.0), axis=0, keepdims=True)
        c_f = lane_sums(rf_ref[...]) * LOG2E
        c_b = lane_sums_back(rb_ref[...]) * LOG2E
        step_f = step_of(rf_ref[...])
        step_b = step_of(rb_ref[...])
        rows_ref[0] = c_f + jnp.log(step_f) * LOG2E
        rows_ref[1] = c_b + jnp.log(step_b) * LOG2E
        high, low = two_parts(own * step_b)
        cols_ref[...] = jnp.concatenate([c_f, c_b, high, low], axis=0).T

    gate = gate_ref[...].astype(F32)
    silu_ref[...] = (gate * jax.nn.sigmoid(gate)).astype(BF16)
    cols = cols_ref[...]
    own = dot(cols.astype(BF16), head_select(j, 4 * H, BLK, 2 * H, 2))
    cols = pltpu.roll(cols, lax.rem(4 * H - HPB * j, 4 * H), 1)
    lane = lax.broadcasted_iota(jnp.int32, (Q, 128), 1)
    for p in range(HPB // 2):
        x = x_ref[:, 128 * p : 128 * (p + 1)]
        halves = []
        for i in (2 * p, 2 * p + 1):
            forward = rows_ref[0, pl.ds(HPB * j + i, 1), :] - cols[:, i : i + 1]
            backward = rows_ref[1, pl.ds(HPB * j + i, 1), :] - cols[:, H + i : H + i + 1]
            w = score_ref[...] * jnp.exp2(jnp.where(s <= t, forward, backward))
            halves.append(dot(w.astype(BF16), x))
        y = jnp.where(lane < HEAD, halves[0], halves[1])
        y = y + own[:, 128 * p : 128 * (p + 1)] * x.astype(F32)
        out_ref[:, 128 * p : 128 * (p + 1)] = y.astype(BF16)


def inside_call(x, gate, rate_f, rate_b, b_f, c_f, b_b, c_b):
    whole = lambda shape: pl.BlockSpec(shape, lambda j: (0,) * len(shape))
    columns = pl.BlockSpec((Q, BLK), lambda j: (0, j))
    return pl.pallas_call(
        inside_kernel,
        grid=(STEPS,),
        in_specs=[columns, columns, whole((H, Q)), whole((H, Q))] + [whole((Q, N))] * 4,
        out_specs=[columns, columns],
        out_shape=[jax.ShapeDtypeStruct((Q, E), BF16)] * 2,
        scratch_shapes=[
            pltpu.VMEM((Q, Q), F32),
            pltpu.VMEM((2, H, Q), F32),
            pltpu.VMEM((Q, 4 * H), F32),
        ],
        cost_estimate=pl.CostEstimate(
            flops=2 * H * Q * Q * 128, bytes_accessed=4 * Q * E * 2, transcendentals=H * Q * Q
        ),
        name="inside_spans",
    )(x, gate, rate_f, rate_b, b_f, c_f, b_b, c_b)


def read_part(ref, index):
    state = ref[index, 0:N, :].astype(F32)
    tail = ref[index, N:ROWS, :].astype(F32)
    return state, tail[0:1] + tail[1:2] + tail[2:3]


def total_kernel(count, copies, place_ref, parts_ref, out_ref):
    backward = place_ref[0]

    def step(i, carried):
        state, kept = carried
        index = jnp.where(backward == 1, count - 1 - i, i)
        own, keep = read_part(parts_ref, index)
        return keep * state + own, keep * kept

    state, kept = lax.fori_loop(
        0, count, step, (jnp.zeros((N, 128), F32), jnp.ones((1, 128), F32)), unroll=4
    )
    high, rest = two_parts(kept)
    middle, low = two_parts(rest)
    row = lax.broadcasted_iota(jnp.int32, (16, 128), 0)
    tail = jnp.where(row == 0, high, jnp.where(row == 1, middle, jnp.where(row == 2, low, 0.0)))
    for g in range(copies):
        out_ref[g, 0:N, :] = state.astype(BF16)
        out_ref[g, N:ROWS, :] = tail.astype(BF16)


def entry_kernel(count, groups, place_ref, totals_ref, parts_ref, out_ref):
    backward, mine = place_ref[0], place_ref[1]

    def outer(i, state):
        index = jnp.where(backward == 1, groups - 1 - i, i)
        own, keep = read_part(totals_ref, index)
        return keep * state + own

    state = lax.fori_loop(0, mine, outer, jnp.zeros((N, 128), F32))

    def step(i, state):
        index = jnp.where(backward == 1, count - 1 - i, i)
        out_ref[index] = state.astype(BF16)
        own, keep = read_part(parts_ref, index)
        return keep * state + own

    lax.fori_loop(0, count, step, state, unroll=4)


def vmem_specs(n):
    return [pl.BlockSpec(memory_space=pltpu.SMEM)] + [pl.BlockSpec(memory_space=pltpu.VMEM)] * n


def final_kernel(
    in_ref, silu_ref, m_ref, rf_ref, rb_ref, cf_ref, cb_ref, gain_ref, w_ref,
    out_ref, scale_ref, acc_ref, square_ref,
):
    j = pl.program_id(0)

    @pl.when(j == 0)
    def _():
        parts = two_parts(jnp.exp(-lane_sums(rf_ref[...])))
        parts += two_parts(jnp.exp(-lane_sums_back(rb_ref[...])))
        scale_ref[...] = jnp.concatenate(parts, axis=0).T.astype(BF16)
        acc_ref[...] = jnp.zeros_like(acc_ref)
        square_ref[...] = jnp.zeros_like(square_ref)

    y = in_ref[...].astype(F32)
    for d, c_ref in enumerate((cf_ref, cb_ref)):
        factor = dot(scale_ref[...], head_select(j, 4 * H, BLK, 2 * H * d, 2))
        m = jnp.concatenate([m_ref[d, k] for k in range(BLK // 128)], axis=1)
        y = y + factor * dot(c_ref[...], m)
    gated = y * silu_ref[...].astype(F32)
    square = gated * gated
    square_ref[...] += square[:, :128] + square[:, 128:]
    acc_ref[...] += dot((gated * gain_ref[...]).astype(BF16), w_ref[...])

    @pl.when(j == STEPS - 1)
    def _():
        mean = jnp.sum(square_ref[...], axis=1, keepdims=True) * (1.0 / E)
        out_ref[...] = (acc_ref[...] * lax.rsqrt(mean + 1e-05)).astype(BF16)


def final_call(inside, silu, m, rate_f, rate_b, c_f, c_b, gain, weight):
    whole = lambda shape: pl.BlockSpec(shape, lambda j: (0,) * len(shape))
    columns = pl.BlockSpec((Q, BLK), lambda j: (0, j))
    return pl.pallas_call(
        final_kernel,
        grid=(STEPS,),
        in_specs=[
            columns,
            columns,
            pl.BlockSpec((2, BLK // 128, N, 128), lambda j: (0, j, 0, 0)),
            whole((H, Q)),
            whole((H, Q)),
            whole((Q, N)),
            whole((Q, N)),
            pl.BlockSpec((1, BLK), lambda j: (0, j)),
            pl.BlockSpec((BLK, D), lambda j: (j, 0)),
        ],
        out_specs=whole((Q, D)),
        out_shape=jax.ShapeDtypeStruct((Q, D), BF16),
        scratch_shapes=[
            pltpu.VMEM((Q, 4 * H), BF16),
            pltpu.VMEM((Q, D), F32),
            pltpu.VMEM((Q, 128), F32),
        ],
        name="gate_norm_project",
    )(inside, silu, m, rate_f, rate_b, c_f, c_b, gain, weight)


def per_device(
    features, gate_input, b_forward, c_forward, b_backward, c_backward,
    rate_forward, rate_backward, norm_gain, out_weight,
):
    count, groups = lax.axis_size("seq"), lax.axis_size("grp")
    states = state_call(features, rate_forward, rate_backward, b_forward, b_backward)
    states = states.reshape(count, ROWS, 128)
    backward = (lax.axis_index("seq") >= count // 2).astype(jnp.int32)
    group = lax.axis_index("grp")
    mine = jnp.where(backward == 1, groups - 1 - group, group)
    place = jnp.stack([backward, mine]).astype(jnp.int32)
    parts = lax.all_to_all(states, "seq", 0, 0, tiled=True)
    totals = pl.pallas_call(
        functools.partial(total_kernel, count, groups),
        in_specs=vmem_specs(1),
        out_specs=pl.BlockSpec(memory_space=pltpu.VMEM),
        out_shape=jax.ShapeDtypeStruct((groups, ROWS, 128), BF16),
        name="group_totals",
    )(place, parts)
    totals = lax.all_to_all(totals, "grp", 0, 0, tiled=True)
    entries = pl.pallas_call(
        functools.partial(entry_kernel, count, groups),
        in_specs=vmem_specs(2),
        out_specs=pl.BlockSpec(memory_space=pltpu.VMEM),
        out_shape=jax.ShapeDtypeStruct((count, N, 128), BF16),
        name="entry_states",
    )(place, totals, parts)
    m = lax.all_to_all(entries, "seq", 0, 0, tiled=True).reshape(2, E // 128, N, 128)
    inside, silu = inside_call(
        features, gate_input, rate_forward, rate_backward,
        b_forward, c_forward, b_backward, c_backward,
    )
    return final_call(
        inside, silu, m, rate_forward, rate_backward, c_forward, c_backward,
        norm_gain.reshape(1, E), out_weight,
    )


def solution(mesh):
    rows = P(("grp", "seq"), None)
    heads = P(None, ("grp", "seq"))
    placed = (rows,) * 6 + (heads, heads, P(), P())
    return jax.shard_map(per_device, mesh=mesh, in_specs=placed, out_specs=rows, check_vma=False)
```

```python
import functools
import jax
import jax.numpy as jnp
from jax import lax
from jax.experimental import pallas as pl
from jax.experimental.pallas import tpu as pltpu
from jax.sharding import PartitionSpec as P

Q = 256
H = 32
HEAD = 64
N = 128
E = 2048
D = 1024
BLK = 256
STEPS = E // BLK
FW = 256
HPB = BLK // HEAD
ROWS = N + 16
LOG2E = 1.4426950408889634
F32 = jnp.float32
BF16 = jnp.bfloat16
LIMIT = pltpu.CompilerParams(vmem_limit_bytes=24 * 1024 * 1024)


def lane_sums(r):
    width = r.shape[1]
    lane = lax.broadcasted_iota(jnp.int32, r.shape, 1)
    shift = 1
    while shift < width:
        r = r + jnp.where(lane >= shift, pltpu.roll(r, shift, 1), 0.0)
        shift *= 2
    return r


def lane_sums_back(r):
    width = r.shape[1]
    lane = lax.broadcasted_iota(jnp.int32, r.shape, 1)
    shift = 1
    while shift < width:
        r = r + jnp.where(lane < width - shift, pltpu.roll(r, width - shift, 1), 0.0)
        shift *= 2
    return r


def step_of(r):
    y = 2.0 * r
    s = jnp.full_like(y, 1.0)
    for k in range(9, 1, -1):
        s = 1.0 - y * (1.0 / k) * s
    return jnp.sqrt(jnp.where(y < 0.5, y * s, 1.0 - jnp.exp(-y)))


def two_parts(a):
    high = a.astype(BF16).astype(F32)
    return high, a - high


def head_select(block, rows, width, first, pairs):
    row = lax.broadcasted_iota(jnp.int32, (rows, width), 0)
    column = lax.broadcasted_iota(jnp.int32, (rows, width), 1)
    head = block * (width // HEAD) + column // HEAD
    hit = (row % H == head) & (row >= first) & (row < first + pairs * H)
    return jnp.where(hit, 1.0, 0.0).astype(BF16)


def dot(a, b):
    return jnp.dot(a, b, preferred_element_type=F32)


def three_rows(value, width):
    high, rest = two_parts(value)
    middle, low = two_parts(rest)
    row = lax.broadcasted_iota(jnp.int32, (16, width), 0)
    tail = jnp.where(row == 0, high, jnp.where(row == 1, middle, jnp.where(row == 2, low, 0.0)))
    return tail.astype(BF16)


def state_kernel(
    x_hbm, rf_hbm, rb_hbm, bf_hbm, bb_hbm, out_ref,
    x_ref, r_ref, b_ref, scale_ref, sems,
):
    copies = [
        pltpu.make_async_copy(rf_hbm, r_ref.at[0], sems.at[0]),
        pltpu.make_async_copy(rb_hbm, r_ref.at[1], sems.at[1]),
        pltpu.make_async_copy(bf_hbm, b_ref.at[0], sems.at[2]),
        pltpu.make_async_copy(bb_hbm, b_ref.at[1], sems.at[3]),
        pltpu.make_async_copy(x_hbm, x_ref, sems.at[4]),
    ]
    for copy in copies:
        copy.start()
    copies[0].wait()
    copies[1].wait()
    parts, keeps = [], []
    for d, sums in enumerate((lane_sums, lane_sums_back)):
        r = r_ref[d]
        c = sums(r)
        total = c[:, Q - 1 : Q] if d == 0 else c[:, 0:1]
        parts += two_parts(step_of(r) * jnp.exp(c - total))
        keeps.append(jnp.broadcast_to(jnp.exp(-total), (H, E)))
    scale_ref[...] = jnp.concatenate(parts, axis=0).T.astype(BF16)
    copies[2].wait()
    copies[3].wait()
    turned = [b_ref[d].astype(F32).T.astype(BF16) for d in range(2)]
    copies[4].wait()
    x = x_ref[...].astype(F32)
    head = lax.broadcasted_iota(jnp.int32, (H, E), 0)
    column = lax.broadcasted_iota(jnp.int32, (H, E), 1)
    for d in range(2):
        factor = dot(scale_ref[...], head_select(0, 4 * H, E, 2 * H * d, 2))
        s = dot(turned[d], (x * factor).astype(BF16)).astype(BF16)
        keep = jnp.where(head == column // HEAD, keeps[d], 0.0)
        tail = three_rows(jnp.sum(keep, axis=0, keepdims=True), E)
        for k in range(E // 128):
            out_ref[d, k, 0:N, :] = s[:, 128 * k : 128 * (k + 1)]
            out_ref[d, k, N:ROWS, :] = tail[:, 128 * k : 128 * (k + 1)]


def state_call(x, rate_f, rate_b, b_f, b_b):
    return pl.pallas_call(
        state_kernel,
        in_specs=[pl.BlockSpec(memory_space=pltpu.HBM)] * 5,
        out_specs=pl.BlockSpec(memory_space=pltpu.VMEM),
        out_shape=jax.ShapeDtypeStruct((2, E // 128, ROWS, 128), BF16),
        scratch_shapes=[
            pltpu.VMEM((Q, E), BF16),
            pltpu.VMEM((2, H, Q), F32),
            pltpu.VMEM((2, Q, N), BF16),
            pltpu.VMEM((Q, 4 * H), BF16),
            pltpu.SemaphoreType.DMA((5,)),
        ],
        compiler_params=LIMIT,
        name="span_states",
    )(x, rate_f, rate_b, b_f, b_b)


def inside_kernel(
    x_ref, gate_ref, rf_ref, rb_ref, bf_ref, cf_ref, bb_ref, cb_ref,
    out_ref, silu_ref, scale_ref, score_ref, rows_ref, cols_ref,
):
    j = pl.program_id(0)
    t = lax.broadcasted_iota(jnp.int32, (Q, Q), 0)
    s = lax.broadcasted_iota(jnp.int32, (Q, Q), 1)

    @pl.when(j == 0)
    def _():
        contract = (((1,), (1,)), ((), ()))
        forward = lax.dot_general(cf_ref[...], bf_ref[...], contract, preferred_element_type=F32)
        backward = lax.dot_general(cb_ref[...], bb_ref[...], contract, preferred_element_type=F32)
        score_ref[...] = jnp.where(s <= t, forward, backward)
        own = jnp.sum(jnp.where(s == t, backward, 0.0), axis=0, keepdims=True)
        c_f = lane_sums(rf_ref[...]) * LOG2E
        c_b = lane_sums_back(rb_ref[...]) * LOG2E
        step_f = step_of(rf_ref[...])
        step_b = step_of(rb_ref[...])
        rows_ref[0] = c_f + jnp.log(step_f) * LOG2E
        rows_ref[1] = c_b + jnp.log(step_b) * LOG2E
        high, low = two_parts(own * step_b)
        cols_ref[...] = jnp.concatenate([c_f, c_b, high, low], axis=0).T
        parts = two_parts(jnp.exp2(-c_f)) + two_parts(jnp.exp2(-c_b))
        scale_ref[...] = jnp.concatenate(parts, axis=0).T.astype(BF16)

    gate = gate_ref[...].astype(F32)
    silu_ref[...] = (gate * jax.nn.sigmoid(gate)).astype(BF16)
    cols = cols_ref[...]
    own = dot(cols.astype(BF16), head_select(j, 4 * H, BLK, 2 * H, 2))
    cols = pltpu.roll(cols, lax.rem(4 * H - HPB * j, 4 * H), 1)
    lane = lax.broadcasted_iota(jnp.int32, (Q, 128), 1)
    for p in range(HPB // 2):
        x = x_ref[:, 128 * p : 128 * (p + 1)]
        halves = []
        for i in (2 * p, 2 * p + 1):
            forward = rows_ref[0, pl.ds(HPB * j + i, 1), :] - cols[:, i : i + 1]
            backward = rows_ref[1, pl.ds(HPB * j + i, 1), :] - cols[:, H + i : H + i + 1]
            w = score_ref[...] * jnp.exp2(jnp.where(s <= t, forward, backward))
            halves.append(dot(w.astype(BF16), x))
        y = jnp.where(lane < HEAD, halves[0], halves[1])
        y = y + own[:, 128 * p : 128 * (p + 1)] * x.astype(F32)
        out_ref[:, 128 * p : 128 * (p + 1)] = y.astype(BF16)


def inside_call(x, gate, rate_f, rate_b, b_f, c_f, b_b, c_b):
    whole = lambda shape: pl.BlockSpec(shape, lambda j: (0,) * len(shape))
    columns = pl.BlockSpec((Q, BLK), lambda j: (0, j))
    return pl.pallas_call(
        inside_kernel,
        grid=(STEPS,),
        in_specs=[columns, columns, whole((H, Q)), whole((H, Q))] + [whole((Q, N))] * 4,
        out_specs=[columns, columns, whole((Q, 4 * H))],
        out_shape=[jax.ShapeDtypeStruct((Q, E), BF16)] * 2
        + [jax.ShapeDtypeStruct((Q, 4 * H), BF16)],
        compiler_params=LIMIT,
        scratch_shapes=[
            pltpu.VMEM((Q, Q), F32),
            pltpu.VMEM((2, H, Q), F32),
            pltpu.VMEM((Q, 4 * H), F32),
        ],
        cost_estimate=pl.CostEstimate(
            flops=2 * H * Q * Q * 128, bytes_accessed=4 * Q * E * 2, transcendentals=H * Q * Q
        ),
        name="inside_spans",
    )(x, gate, rate_f, rate_b, b_f, c_f, b_b, c_b)


def read_part(ref, index):
    state = ref[index, 0:N, :].astype(F32)
    tail = ref[index, N:ROWS, :].astype(F32)
    return state, tail[0:1] + tail[1:2] + tail[2:3]


def total_kernel(count, copies, place_ref, parts_ref, out_ref):
    backward = place_ref[0]

    def step(i, carried):
        state, kept = carried
        index = jnp.where(backward == 1, count - 1 - i, i)
        own, keep = read_part(parts_ref, index)
        return keep * state + own, keep * kept

    state, kept = lax.fori_loop(
        0, count, step, (jnp.zeros((N, 128), F32), jnp.ones((1, 128), F32)), unroll=4
    )
    tail = three_rows(kept, 128)
    for g in range(copies):
        out_ref[g, 0:N, :] = state.astype(BF16)
        out_ref[g, N:ROWS, :] = tail


def entry_kernel(count, groups, place_ref, totals_ref, parts_ref, out_ref):
    backward, mine = place_ref[0], place_ref[1]

    def outer(i, state):
        index = jnp.where(backward == 1, groups - 1 - i, i)
        own, keep = read_part(totals_ref, index)
        return keep * state + own

    state = lax.fori_loop(0, mine, outer, jnp.zeros((N, 128), F32))

    def step(i, state):
        index = jnp.where(backward == 1, count - 1 - i, i)
        out_ref[index] = state.astype(BF16)
        own, keep = read_part(parts_ref, index)
        return keep * state + own

    lax.fori_loop(0, count, step, state, unroll=4)


def vmem_specs(n):
    return [pl.BlockSpec(memory_space=pltpu.SMEM)] + [pl.BlockSpec(memory_space=pltpu.VMEM)] * n


def final_kernel(
    in_ref, silu_ref, scale_ref, m_ref, cf_ref, cb_ref, gain_ref, w_ref, out_ref, normed_ref
):
    square = jnp.zeros((Q, 128), F32)
    for j in range(E // FW):
        at = pl.ds(FW * j, FW)
        y = in_ref[:, at].astype(F32)
        for d, c_ref in enumerate((cf_ref, cb_ref)):
            factor = dot(scale_ref[...], head_select(j, 4 * H, FW, 2 * H * d, 2))
            m = jnp.concatenate([m_ref[d, FW // 128 * j + k] for k in range(FW // 128)], axis=1)
            y = y + factor * dot(c_ref[...], m)
        gated = y * silu_ref[:, at].astype(F32)
        for k in range(FW // 128):
            part = gated[:, 128 * k : 128 * (k + 1)]
            square = square + part * part
        normed_ref[:, at] = (gated * gain_ref[:, at]).astype(BF16)
    mean = jnp.sum(square, axis=1, keepdims=True) * (1.0 / E)
    scale = lax.rsqrt(mean + 1e-05)
    for n in range(D // 256):
        at = pl.ds(256 * n, 256)
        out_ref[:, at] = (dot(normed_ref[...], w_ref[:, at]) * scale).astype(BF16)


def final_call(inside, silu, scale, m, c_f, c_b, gain, weight):
    return pl.pallas_call(
        final_kernel,
        in_specs=[pl.BlockSpec(memory_space=pltpu.VMEM)] * 8,
        out_specs=pl.BlockSpec(memory_space=pltpu.VMEM),
        out_shape=jax.ShapeDtypeStruct((Q, D), BF16),
        scratch_shapes=[pltpu.VMEM((Q, E), BF16)],
        compiler_params=LIMIT,
        name="gate_norm_project",
    )(inside, silu, scale, m, c_f, c_b, gain, weight)


def per_device(
    features, gate_input, b_forward, c_forward, b_backward, c_backward,
    rate_forward, rate_backward, norm_gain, out_weight,
):
    count, groups = lax.axis_size("seq"), lax.axis_size("grp")
    states = state_call(features, rate_forward, rate_backward, b_forward, b_backward)
    states = states.reshape(count, ROWS, 128)
    backward = (lax.axis_index("seq") >= count // 2).astype(jnp.int32)
    group = lax.axis_index("grp")
    mine = jnp.where(backward == 1, groups - 1 - group, group)
    place = jnp.stack([backward, mine]).astype(jnp.int32)
    parts = lax.all_to_all(states, "seq", 0, 0, tiled=True)
    totals = pl.pallas_call(
        functools.partial(total_kernel, count, groups),
        in_specs=vmem_specs(1),
        out_specs=pl.BlockSpec(memory_space=pltpu.VMEM),
        out_shape=jax.ShapeDtypeStruct((groups, ROWS, 128), BF16),
        compiler_params=LIMIT,
        name="group_totals",
    )(place, parts)
    totals = lax.all_to_all(totals, "grp", 0, 0, tiled=True)
    entries = pl.pallas_call(
        functools.partial(entry_kernel, count, groups),
        in_specs=vmem_specs(2),
        out_specs=pl.BlockSpec(memory_space=pltpu.VMEM),
        out_shape=jax.ShapeDtypeStruct((count, N, 128), BF16),
        compiler_params=LIMIT,
        name="entry_states",
    )(place, totals, parts)
    m = lax.all_to_all(entries, "seq", 0, 0, tiled=True).reshape(2, E // 128, N, 128)
    inside, silu, scale = inside_call(
        features, gate_input, rate_forward, rate_backward,
        b_forward, c_forward, b_backward, c_backward,
    )
    return final_call(
        inside, silu, scale, m, c_forward, c_backward, norm_gain.reshape(1, E), out_weight
    )


def solution(mesh):
    rows = P(("grp", "seq"), None)
    heads = P(None, ("grp", "seq"))
    placed = (rows,) * 6 + (heads, heads, P(), P())
    return jax.shard_map(per_device, mesh=mesh, in_specs=placed, out_specs=rows, check_vma=False)
```

```python
import functools
import jax
import jax.numpy as jnp
from jax import lax
from jax.experimental import pallas as pl
from jax.experimental.pallas import tpu as pltpu
from jax.sharding import PartitionSpec as P

Q = 256
H = 32
HEAD = 64
N = 128
E = 2048
D = 1024
BLK = 256
STEPS = E // BLK
FW = 256
HPB = BLK // HEAD
ROWS = N + 16
HALF = E // 2
SHARE = N // 2
PART = SHARE + 16
LOG2E = 1.4426950408889634
F32 = jnp.float32
BF16 = jnp.bfloat16
LIMIT = pltpu.CompilerParams(vmem_limit_bytes=24 * 1024 * 1024)


def lane_sums(r):
    width = r.shape[1]
    lane = lax.broadcasted_iota(jnp.int32, r.shape, 1)
    shift = 1
    while shift < width:
        r = r + jnp.where(lane >= shift, pltpu.roll(r, shift, 1), 0.0)
        shift *= 2
    return r


def lane_sums_back(r):
    width = r.shape[1]
    lane = lax.broadcasted_iota(jnp.int32, r.shape, 1)
    shift = 1
    while shift < width:
        r = r + jnp.where(lane < width - shift, pltpu.roll(r, width - shift, 1), 0.0)
        shift *= 2
    return r


def step_of(r):
    y = 2.0 * r
    s = jnp.full_like(y, 1.0)
    for k in range(9, 1, -1):
        s = 1.0 - y * (1.0 / k) * s
    return jnp.sqrt(jnp.where(y < 0.5, y * s, 1.0 - jnp.exp(-y)))


def two_parts(a):
    high = a.astype(BF16).astype(F32)
    return high, a - high


def head_select(block, rows, width, first, pairs):
    row = lax.broadcasted_iota(jnp.int32, (rows, width), 0)
    column = lax.broadcasted_iota(jnp.int32, (rows, width), 1)
    head = block * (width // HEAD) + column // HEAD
    hit = (row % H == head) & (row >= first) & (row < first + pairs * H)
    return jnp.where(hit, 1.0, 0.0).astype(BF16)


def dot(a, b):
    return jnp.dot(a, b, preferred_element_type=F32)


def three_rows(value, width):
    high, rest = two_parts(value)
    middle, low = two_parts(rest)
    row = lax.broadcasted_iota(jnp.int32, (16, width), 0)
    tail = jnp.where(row == 0, high, jnp.where(row == 1, middle, jnp.where(row == 2, low, 0.0)))
    return tail.astype(BF16)


def state_kernel(
    place_ref, x_hbm, rf_hbm, rb_hbm, bf_hbm, bb_hbm, own_ref, next_ref, last_ref,
    x_ref, r_ref, b_ref, scale_ref, keep_ref, sems,
):
    copies = [
        pltpu.make_async_copy(rf_hbm, r_ref.at[0], sems.at[0]),
        pltpu.make_async_copy(rb_hbm, r_ref.at[1], sems.at[1]),
        pltpu.make_async_copy(bf_hbm, b_ref.at[0], sems.at[2]),
        pltpu.make_async_copy(bb_hbm, b_ref.at[1], sems.at[3]),
        pltpu.make_async_copy(x_hbm, x_ref, sems.at[4]),
    ]
    for copy in copies:
        copy.start()
    odd = place_ref[0]
    copies[0].wait()
    copies[1].wait()
    parts = []
    for d, sums in enumerate((lane_sums, lane_sums_back)):
        r = r_ref[d]
        c = sums(r)
        total = c[:, Q - 1 : Q] if d == 0 else c[:, 0:1]
        parts += two_parts(step_of(r) * jnp.exp(c - total))
        keep_ref[d] = jnp.broadcast_to(jnp.exp(-total), (H, HALF))
    scale_ref[...] = jnp.concatenate(parts, axis=0).T.astype(BF16)
    copies[2].wait()
    copies[3].wait()
    turned = [b_ref[d].astype(F32).T.astype(BF16) for d in range(2)]
    copies[4].wait()
    head = lax.broadcasted_iota(jnp.int32, (H, HALF), 0)
    column = lax.broadcasted_iota(jnp.int32, (H, HALF), 1)

    work = ((0, odd, next_ref), (1, 1 - odd, last_ref), (0, 1 - odd, own_ref.at[0]), (1, odd, own_ref.at[1]))
    for d, half, ref in work:
        at = pl.multiple_of(half * HALF, HALF)
        x = x_ref[:, pl.ds(at, HALF)].astype(F32)
        factor = dot(scale_ref[...], head_select(half, 4 * H, HALF, 2 * H * d, 2))
        s = dot(turned[d], (x * factor).astype(BF16)).astype(BF16)
        keep = jnp.where(head == half * (H // 2) + column // HEAD, keep_ref[d], 0.0)
        tail = three_rows(jnp.sum(keep, axis=0, keepdims=True), HALF)
        for k in range(HALF // 128):
            ref[k, 0:N, :] = s[:, 128 * k : 128 * (k + 1)]
            ref[k, N:ROWS, :] = tail[:, 128 * k : 128 * (k + 1)]


def state_call(place, x, rate_f, rate_b, b_f, b_b):
    part = jax.ShapeDtypeStruct((HALF // 128, ROWS, 128), BF16)
    return pl.pallas_call(
        state_kernel,
        in_specs=[pl.BlockSpec(memory_space=pltpu.SMEM)]
        + [pl.BlockSpec(memory_space=pltpu.HBM)] * 5,
        out_specs=[pl.BlockSpec(memory_space=pltpu.VMEM)] * 3,
        out_shape=[jax.ShapeDtypeStruct((2, HALF // 128, ROWS, 128), BF16), part, part],
        scratch_shapes=[
            pltpu.VMEM((Q, E), BF16),
            pltpu.VMEM((2, H, Q), F32),
            pltpu.VMEM((2, Q, N), BF16),
            pltpu.VMEM((Q, 4 * H), BF16),
            pltpu.VMEM((2, H, HALF), F32),
            pltpu.SemaphoreType.DMA((5,)),
        ],
        compiler_params=pltpu.CompilerParams(vmem_limit_bytes=60 * 1024 * 1024),
        name="span_states",
    )(place, x, rate_f, rate_b, b_f, b_b)


def pair_kernel(own_ref, from_last_ref, from_next_ref, out_ref):
    for d, first_ref in enumerate((from_last_ref, from_next_ref)):
        for k in range(HALF // 128):
            second, keep = read_part(own_ref.at[d], k, N)
            first, first_keep = read_part(first_ref, k, N)
            total = (keep * first + second).astype(BF16)
            tail = three_rows(keep * first_keep, 128)
            for n in range(2):
                place = (d * (HALF // 128) + k) * 2 + n
                out_ref[place, 0:SHARE, :] = total[SHARE * n : SHARE * (n + 1)]
                out_ref[place, SHARE:PART, :] = tail


def pair_call(own, from_last, from_next):
    return pl.pallas_call(
        pair_kernel,
        in_specs=[pl.BlockSpec(memory_space=pltpu.VMEM)] * 3,
        out_specs=pl.BlockSpec(memory_space=pltpu.VMEM),
        out_shape=jax.ShapeDtypeStruct((2 * E // 128, PART, 128), BF16),
        compiler_params=LIMIT,
        name="pair_totals",
    )(own, from_last, from_next)


def inside_kernel(
    x_ref, gate_ref, rf_ref, rb_ref, bf_ref, cf_ref, bb_ref, cb_ref, w_ref,
    out_ref, silu_ref, scale_ref, score_ref, rows_ref, cols_ref,
):
    j = pl.program_id(0)
    t = lax.broadcasted_iota(jnp.int32, (Q, Q), 0)
    s = lax.broadcasted_iota(jnp.int32, (Q, Q), 1)

    @pl.when(j == 0)
    def _():
        contract = (((1,), (1,)), ((), ()))
        forward = lax.dot_general(cf_ref[...], bf_ref[...], contract, preferred_element_type=F32)
        backward = lax.dot_general(cb_ref[...], bb_ref[...], contract, preferred_element_type=F32)
        score_ref[...] = jnp.where(s <= t, forward, backward)
        own = jnp.sum(jnp.where(s == t, backward, 0.0), axis=0, keepdims=True)
        c_f = lane_sums(rf_ref[...]) * LOG2E
        c_b = lane_sums_back(rb_ref[...]) * LOG2E
        step_f = step_of(rf_ref[...])
        step_b = step_of(rb_ref[...])
        rows_ref[0] = c_f + jnp.log(step_f) * LOG2E
        rows_ref[1] = c_b + jnp.log(step_b) * LOG2E
        high, low = two_parts(own * step_b)
        cols_ref[...] = jnp.concatenate([c_f, c_b, high, low], axis=0).T
        parts = two_parts(jnp.exp2(-c_f)) + two_parts(jnp.exp2(-c_b))
        scale_ref[...] = jnp.concatenate(parts, axis=0).T.astype(BF16)

    gate = gate_ref[...].astype(F32)
    silu_ref[...] = (gate * jax.nn.sigmoid(gate)).astype(BF16)
    cols = cols_ref[...]
    own = dot(cols.astype(BF16), head_select(j, 4 * H, BLK, 2 * H, 2))
    cols = pltpu.roll(cols, lax.rem(4 * H - HPB * j, 4 * H), 1)
    lane = lax.broadcasted_iota(jnp.int32, (Q, 128), 1)
    for p in range(HPB // 2):
        x = x_ref[:, 128 * p : 128 * (p + 1)]
        halves = []
        for i in (2 * p, 2 * p + 1):
            forward = rows_ref[0, pl.ds(HPB * j + i, 1), :] - cols[:, i : i + 1]
            backward = rows_ref[1, pl.ds(HPB * j + i, 1), :] - cols[:, H + i : H + i + 1]
            w = score_ref[...] * jnp.exp2(jnp.where(s <= t, forward, backward))
            halves.append(dot(w.astype(BF16), x))
        y = jnp.where(lane < HEAD, halves[0], halves[1])
        y = y + own[:, 128 * p : 128 * (p + 1)] * x.astype(F32)
        out_ref[:, 128 * p : 128 * (p + 1)] = y.astype(BF16)


def inside_call(x, gate, rate_f, rate_b, b_f, c_f, b_b, c_b, weight):
    whole = lambda shape: pl.BlockSpec(shape, lambda j: (0,) * len(shape))
    columns = pl.BlockSpec((Q, BLK), lambda j: (0, j))
    return pl.pallas_call(
        inside_kernel,
        grid=(STEPS,),
        in_specs=[columns, columns, whole((H, Q)), whole((H, Q))] + [whole((Q, N))] * 4
        + [pl.BlockSpec(memory_space=pltpu.VMEM)],
        out_specs=[columns, columns, whole((Q, 4 * H))],
        out_shape=[jax.ShapeDtypeStruct((Q, E), BF16)] * 2
        + [jax.ShapeDtypeStruct((Q, 4 * H), BF16)],
        compiler_params=LIMIT,
        scratch_shapes=[
            pltpu.VMEM((Q, Q), F32),
            pltpu.VMEM((2, H, Q), F32),
            pltpu.VMEM((Q, 4 * H), F32),
        ],
        cost_estimate=pl.CostEstimate(
            flops=2 * H * Q * Q * 128, bytes_accessed=4 * Q * E * 2, transcendentals=H * Q * Q
        ),
        name="inside_spans",
    )(x, gate, rate_f, rate_b, b_f, c_f, b_b, c_b, weight)


def read_part(ref, index, rows):
    state = ref[index, 0:rows, :].astype(F32)
    tail = ref[index, rows : rows + 16, :].astype(F32)
    return state, tail[0:1] + tail[1:2] + tail[2:3]


def total_kernel(count, copies, place_ref, parts_ref, out_ref):
    backward = place_ref[1]

    def step(i, carried):
        pair = jnp.where(backward == 1, count // 2 - 1 - i, i)
        result = []
        for q in range(2):
            own, keep = read_part(parts_ref, 2 * pair + q, SHARE)
            result += [keep * carried[2 * q] + own, keep * carried[2 * q + 1]]
        return tuple(result)

    start = (jnp.zeros((SHARE, 128), F32), jnp.ones((1, 128), F32))
    result = lax.fori_loop(0, count // 2, step, start + start, unroll=4)
    for q in range(2):
        state = result[2 * q].astype(BF16)
        tail = three_rows(result[2 * q + 1], 128)
        for g in range(copies):
            out_ref[g, PART * q : PART * q + SHARE, :] = state
            out_ref[g, PART * q + SHARE : PART * (q + 1), :] = tail


def entry_kernel(count, groups, place_ref, totals_ref, parts_ref, out_ref):
    backward, mine = place_ref[1], place_ref[2]
    states = []
    for q in range(2):
        def outer(i, state, q=q):
            index = jnp.where(backward == 1, groups - 1 - i, i)
            own = totals_ref[index, PART * q : PART * q + SHARE, :].astype(F32)
            tail = totals_ref[index, PART * q + SHARE : PART * (q + 1), :].astype(F32)
            return (tail[0:1] + tail[1:2] + tail[2:3]) * state + own

        open_pair = (mine == 0) & (backward == q)
        limit = jnp.where(open_pair, groups, mine)
        states.append(lax.fori_loop(0, limit, outer, jnp.zeros((SHARE, 128), F32)))

    def step(i, states):
        pair = jnp.where(backward == 1, count // 2 - 1 - i, i)
        result = []
        for q in range(2):
            out_ref[2 * pair + q] = states[q].astype(BF16)
            own, keep = read_part(parts_ref, 2 * pair + q, SHARE)
            result.append(keep * states[q] + own)
        return tuple(result)

    lax.fori_loop(0, count // 2, step, tuple(states), unroll=4)


def vmem_specs(n):
    return [pl.BlockSpec(memory_space=pltpu.SMEM)] + [pl.BlockSpec(memory_space=pltpu.VMEM)] * n


def final_kernel(
    place_ref, in_ref, silu_ref, scale_ref, pair_ref, from_last_ref, from_next_ref,
    other_f_ref, other_b_ref, cf_ref, cb_ref, gain_ref, w_ref, out_ref, normed_ref, m_ref,
):
    odd = place_ref[0]
    blocks = HALF // 128
    others = (other_f_ref, other_b_ref)
    for d, first_ref in enumerate((from_last_ref, from_next_ref)):
        half = 1 - odd if d == 0 else odd
        for k in range(blocks):
            first, keep = read_part(first_ref, k, N)
            entry = keep * pair_ref[d, k].astype(F32) + first
            m_ref[d, half * blocks + k] = entry.astype(BF16)
            m_ref[d, (1 - half) * blocks + k] = others[d][k]
    square = jnp.zeros((Q, 128), F32)
    for j in range(E // FW):
        at = pl.ds(FW * j, FW)
        y = in_ref[:, at].astype(F32)
        for d, c_ref in enumerate((cf_ref, cb_ref)):
            factor = dot(scale_ref[...], head_select(j, 4 * H, FW, 2 * H * d, 2))
            m = jnp.concatenate([m_ref[d, FW // 128 * j + k] for k in range(FW // 128)], axis=1)
            y = y + factor * dot(c_ref[...], m)
        gated = y * silu_ref[:, at].astype(F32)
        for k in range(FW // 128):
            part = gated[:, 128 * k : 128 * (k + 1)]
            square = square + part * part
        normed_ref[:, at] = (gated * gain_ref[:, at]).astype(BF16)
    mean = jnp.sum(square, axis=1, keepdims=True) * (1.0 / E)
    scale = lax.rsqrt(mean + 1e-05)
    for n in range(D // 256):
        at = pl.ds(256 * n, 256)
        out_ref[:, at] = (dot(normed_ref[...], w_ref[:, at]) * scale).astype(BF16)


def final_call(place, inside, silu, scale, states, c_f, c_b, gain, weight):
    return pl.pallas_call(
        final_kernel,
        in_specs=vmem_specs(12),
        out_specs=pl.BlockSpec(memory_space=pltpu.VMEM),
        out_shape=jax.ShapeDtypeStruct((Q, D), BF16),
        scratch_shapes=[
            pltpu.VMEM((Q, E), BF16),
            pltpu.VMEM((2, E // 128, N, 128), BF16),
        ],
        compiler_params=LIMIT,
        name="gate_norm_project",
    )(place, inside, silu, scale, *states, c_f, c_b, gain, weight)


def per_device(
    features, gate_input, b_forward, c_forward, b_backward, c_backward,
    rate_forward, rate_backward, norm_gain, out_weight,
):
    count, groups = lax.axis_size("seq"), lax.axis_size("grp")
    member, group = lax.axis_index("seq"), lax.axis_index("grp")
    odd = member % 2
    backward = (member >= count // 2).astype(jnp.int32)
    mine = jnp.where(backward == 1, groups - 1 - group, group)
    place = jnp.stack([odd, backward, mine]).astype(jnp.int32)
    spans = count * groups
    up = [(k, k + 1) for k in range(spans)]
    down = [(k, k - 1) for k in range(spans)]
    own, to_next, to_last = state_call(
        place, features, rate_forward, rate_backward, b_forward, b_backward
    )
    from_last = lax.ppermute(to_next, ("grp", "seq"), up[:-1])
    from_next = lax.ppermute(to_last, ("grp", "seq"), down[1:])
    parts = pair_call(own, from_last, from_next)
    parts = lax.all_to_all(parts, "seq", 0, 0, tiled=True)
    totals = pl.pallas_call(
        functools.partial(total_kernel, count, groups),
        in_specs=vmem_specs(1),
        out_specs=pl.BlockSpec(memory_space=pltpu.VMEM),
        out_shape=jax.ShapeDtypeStruct((groups, 2 * PART, 128), BF16),
        compiler_params=LIMIT,
        name="group_totals",
    )(place, parts)
    totals = lax.all_to_all(totals, "grp", 0, 0, tiled=True)
    entries = pl.pallas_call(
        functools.partial(entry_kernel, count, groups),
        in_specs=vmem_specs(2),
        out_specs=pl.BlockSpec(memory_space=pltpu.VMEM),
        out_shape=jax.ShapeDtypeStruct((count, SHARE, 128), BF16),
        compiler_params=LIMIT,
        name="entry_states",
    )(place, totals, parts)
    pair = lax.all_to_all(entries, "seq", 0, 0, tiled=True)
    pair = pair.reshape(2, HALF // 128, N, 128)
    other_f = lax.ppermute(pair[0], ("grp", "seq"), down[1:] + [(0, spans - 1)])
    other_b = lax.ppermute(pair[1], ("grp", "seq"), up[:-1] + [(spans - 1, 0)])
    inside, silu, scale = inside_call(
        features, gate_input, rate_forward, rate_backward,
        b_forward, c_forward, b_backward, c_backward, out_weight,
    )
    states = (pair, from_last, from_next, other_f, other_b)
    return final_call(
        place, inside, silu, scale, states, c_forward, c_backward,
        norm_gain.reshape(1, E), out_weight,
    )


def solution(mesh):
    rows = P(("grp", "seq"), None)
    heads = P(None, ("grp", "seq"))
    placed = (rows,) * 6 + (heads, heads, P(), P())
    return jax.shard_map(per_device, mesh=mesh, in_specs=placed, out_specs=rows, check_vma=False)
```

```python
import functools
import jax
import jax.numpy as jnp
from jax import lax
from jax.experimental import pallas as pl
from jax.experimental.pallas import tpu as pltpu
from jax.sharding import PartitionSpec as P

Q = 256
H = 32
HEAD = 64
N = 128
E = 2048
D = 1024
BLK = 256
STEPS = E // BLK
FW = 256
HPB = BLK // HEAD
ROWS = N + 16
LOG2E = 1.4426950408889634
F32 = jnp.float32
BF16 = jnp.bfloat16
LIMIT = pltpu.CompilerParams(vmem_limit_bytes=24 * 1024 * 1024)


def lane_sums(r):
    width = r.shape[1]
    lane = lax.broadcasted_iota(jnp.int32, r.shape, 1)
    shift = 1
    while shift < width:
        r = r + jnp.where(lane >= shift, pltpu.roll(r, shift, 1), 0.0)
        shift *= 2
    return r


def lane_sums_back(r):
    width = r.shape[1]
    lane = lax.broadcasted_iota(jnp.int32, r.shape, 1)
    shift = 1
    while shift < width:
        r = r + jnp.where(lane < width - shift, pltpu.roll(r, width - shift, 1), 0.0)
        shift *= 2
    return r


def step_of(r):
    y = 2.0 * r
    s = jnp.full_like(y, 1.0)
    for k in range(9, 1, -1):
        s = 1.0 - y * (1.0 / k) * s
    return jnp.sqrt(jnp.where(y < 0.5, y * s, 1.0 - jnp.exp(-y)))


def two_parts(a):
    high = a.astype(BF16).astype(F32)
    return high, a - high


def head_select(block, rows, width, first, pairs):
    row = lax.broadcasted_iota(jnp.int32, (rows, width), 0)
    column = lax.broadcasted_iota(jnp.int32, (rows, width), 1)
    head = block * (width // HEAD) + column // HEAD
    hit = (row % H == head) & (row >= first) & (row < first + pairs * H)
    return jnp.where(hit, 1.0, 0.0).astype(BF16)


def dot(a, b):
    return jnp.dot(a, b, preferred_element_type=F32)


def three_rows(value, width):
    high, rest = two_parts(value)
    middle, low = two_parts(rest)
    row = lax.broadcasted_iota(jnp.int32, (16, width), 0)
    tail = jnp.where(row == 0, high, jnp.where(row == 1, middle, jnp.where(row == 2, low, 0.0)))
    return tail.astype(BF16)


def state_kernel(
    x_hbm, rf_hbm, rb_hbm, bf_hbm, bb_hbm, out_ref, total_ref,
    x_ref, r_ref, b_ref, scale_ref, sems,
):
    copies = [
        pltpu.make_async_copy(rf_hbm, r_ref.at[0], sems.at[0]),
        pltpu.make_async_copy(rb_hbm, r_ref.at[1], sems.at[1]),
        pltpu.make_async_copy(bf_hbm, b_ref.at[0], sems.at[2]),
        pltpu.make_async_copy(bb_hbm, b_ref.at[1], sems.at[3]),
        pltpu.make_async_copy(x_hbm, x_ref, sems.at[4]),
    ]
    for copy in copies:
        copy.start()
    copies[0].wait()
    copies[1].wait()
    row = lax.broadcasted_iota(jnp.int32, (H, 128), 0)
    lane = lax.broadcasted_iota(jnp.int32, (H, 128), 1)
    parts, totals = [], 0.0
    for d, sums in enumerate((lane_sums, lane_sums_back)):
        r = r_ref[d]
        c = sums(r)
        total = c[:, Q - 1 : Q] if d == 0 else c[:, 0:1]
        parts += two_parts(step_of(r) * jnp.exp(c - total))
        totals = totals + jnp.where(lane == row + H * d, total, 0.0)
    total_ref[...] = jnp.sum(totals, axis=0, keepdims=True)
    scale_ref[...] = jnp.concatenate(parts, axis=0).T.astype(BF16)
    copies[2].wait()
    copies[3].wait()
    turned = [b_ref[d].astype(F32).T.astype(BF16) for d in range(2)]
    copies[4].wait()
    x = x_ref[...].astype(F32)
    for d in range(2):
        factor = dot(scale_ref[...], head_select(0, 4 * H, E, 2 * H * d, 2))
        s = dot(turned[d], (x * factor).astype(BF16)).astype(BF16)
        for k in range(E // 128):
            out_ref[d, k] = s[:, 128 * k : 128 * (k + 1)]


def state_call(x, rate_f, rate_b, b_f, b_b):
    return pl.pallas_call(
        state_kernel,
        in_specs=[pl.BlockSpec(memory_space=pltpu.HBM)] * 5,
        out_specs=[pl.BlockSpec(memory_space=pltpu.VMEM)] * 2,
        out_shape=[
            jax.ShapeDtypeStruct((2, E // 128, N, 128), BF16),
            jax.ShapeDtypeStruct((1, 128), F32),
        ],
        scratch_shapes=[
            pltpu.VMEM((Q, E), BF16),
            pltpu.VMEM((2, H, Q), F32),
            pltpu.VMEM((2, Q, N), BF16),
            pltpu.VMEM((Q, 4 * H), BF16),
            pltpu.SemaphoreType.DMA((5,)),
        ],
        compiler_params=pltpu.CompilerParams(vmem_limit_bytes=60 * 1024 * 1024),
        name="span_states",
    )(x, rate_f, rate_b, b_f, b_b)


def inside_kernel(
    x_ref, gate_ref, rf_ref, rb_ref, bf_ref, cf_ref, bb_ref, cb_ref, w_ref,
    out_ref, silu_ref, scale_ref, score_ref, rows_ref, cols_ref,
):
    j = pl.program_id(0)
    t = lax.broadcasted_iota(jnp.int32, (Q, Q), 0)
    s = lax.broadcasted_iota(jnp.int32, (Q, Q), 1)

    @pl.when(j == 0)
    def _():
        contract = (((1,), (1,)), ((), ()))
        forward = lax.dot_general(cf_ref[...], bf_ref[...], contract, preferred_element_type=F32)
        backward = lax.dot_general(cb_ref[...], bb_ref[...], contract, preferred_element_type=F32)
        score_ref[...] = jnp.where(s <= t, forward, backward)
        own = jnp.sum(jnp.where(s == t, backward, 0.0), axis=0, keepdims=True)
        c_f = lane_sums(rf_ref[...]) * LOG2E
        c_b = lane_sums_back(rb_ref[...]) * LOG2E
        step_f = step_of(rf_ref[...])
        step_b = step_of(rb_ref[...])
        rows_ref[0] = c_f + jnp.log(step_f) * LOG2E
        rows_ref[1] = c_b + jnp.log(step_b) * LOG2E
        high, low = two_parts(own * step_b)
        cols_ref[...] = jnp.concatenate([c_f, c_b, high, low], axis=0).T
        parts = two_parts(jnp.exp2(-c_f)) + two_parts(jnp.exp2(-c_b))
        scale_ref[...] = jnp.concatenate(parts, axis=0).T.astype(BF16)

    gate = gate_ref[...].astype(F32)
    silu_ref[...] = (gate * jax.nn.sigmoid(gate)).astype(BF16)
    cols = cols_ref[...]
    own = dot(cols.astype(BF16), head_select(j, 4 * H, BLK, 2 * H, 2))
    cols = pltpu.roll(cols, lax.rem(4 * H - HPB * j, 4 * H), 1)
    lane = lax.broadcasted_iota(jnp.int32, (Q, 128), 1)
    for p in range(HPB // 2):
        x = x_ref[:, 128 * p : 128 * (p + 1)]
        halves = []
        for i in (2 * p, 2 * p + 1):
            forward = rows_ref[0, pl.ds(HPB * j + i, 1), :] - cols[:, i : i + 1]
            backward = rows_ref[1, pl.ds(HPB * j + i, 1), :] - cols[:, H + i : H + i + 1]
            w = score_ref[...] * jnp.exp2(jnp.where(s <= t, forward, backward))
            halves.append(dot(w.astype(BF16), x))
        y = jnp.where(lane < HEAD, halves[0], halves[1])
        y = y + own[:, 128 * p : 128 * (p + 1)] * x.astype(F32)
        out_ref[:, 128 * p : 128 * (p + 1)] = y.astype(BF16)


def inside_call(x, gate, rate_f, rate_b, b_f, c_f, b_b, c_b, weight):
    whole = lambda shape: pl.BlockSpec(shape, lambda j: (0,) * len(shape))
    columns = pl.BlockSpec((Q, BLK), lambda j: (0, j))
    return pl.pallas_call(
        inside_kernel,
        grid=(STEPS,),
        in_specs=[columns, columns, whole((H, Q)), whole((H, Q))] + [whole((Q, N))] * 4
        + [pl.BlockSpec(memory_space=pltpu.VMEM)],
        out_specs=[columns, columns, whole((Q, 4 * H))],
        out_shape=[jax.ShapeDtypeStruct((Q, E), BF16)] * 2
        + [jax.ShapeDtypeStruct((Q, 4 * H), BF16)],
        compiler_params=LIMIT,
        scratch_shapes=[
            pltpu.VMEM((Q, Q), F32),
            pltpu.VMEM((2, H, Q), F32),
            pltpu.VMEM((Q, 4 * H), F32),
        ],
        cost_estimate=pl.CostEstimate(
            flops=2 * H * Q * Q * 128, bytes_accessed=4 * Q * E * 2, transcendentals=H * Q * Q
        ),
        name="inside_spans",
    )(x, gate, rate_f, rate_b, b_f, c_f, b_b, c_b, weight)


def read_part(ref, index):
    state = ref[index, 0:N, :].astype(F32)
    tail = ref[index, N:ROWS, :].astype(F32)
    return state, tail[0:1] + tail[1:2] + tail[2:3]


def owned_decays(first, logs_ref, keep_ref):
    lane = lax.broadcasted_iota(jnp.int32, logs_ref.shape, 1)
    logs = logs_ref[...]
    low = jnp.sum(jnp.where(lane == first, logs, 0.0), axis=1, keepdims=True)
    high = jnp.sum(jnp.where(lane == first + 1, logs, 0.0), axis=1, keepdims=True)
    keep_ref[...] = jnp.exp(-jnp.where(lane < HEAD, low, high))


def total_kernel(count, copies, place_ref, logs_ref, parts_ref, out_ref, keep_ref):
    backward = place_ref[0]
    owned_decays(place_ref[2], logs_ref, keep_ref)

    def step(i, carried):
        state, kept = carried
        index = jnp.where(backward == 1, count - 1 - i, i)
        keep = keep_ref[pl.ds(index, 1), :]
        return keep * state + parts_ref[index].astype(F32), keep * kept

    state, kept = lax.fori_loop(
        0, count, step, (jnp.zeros((N, 128), F32), jnp.ones((1, 128), F32)), unroll=4
    )
    tail = three_rows(kept, 128)
    for g in range(copies):
        out_ref[g, 0:N, :] = state.astype(BF16)
        out_ref[g, N:ROWS, :] = tail


def entry_kernel(count, groups, place_ref, totals_ref, logs_ref, parts_ref, out_ref, keep_ref):
    backward, mine = place_ref[0], place_ref[1]
    owned_decays(place_ref[2], logs_ref, keep_ref)

    def outer(i, state):
        index = jnp.where(backward == 1, groups - 1 - i, i)
        own, keep = read_part(totals_ref, index)
        return keep * state + own

    state = lax.fori_loop(0, mine, outer, jnp.zeros((N, 128), F32))

    def step(i, state):
        index = jnp.where(backward == 1, count - 1 - i, i)
        out_ref[index] = state.astype(BF16)
        return keep_ref[pl.ds(index, 1), :] * state + parts_ref[index].astype(F32)

    lax.fori_loop(0, count, step, state, unroll=4)


def vmem_specs(n):
    return [pl.BlockSpec(memory_space=pltpu.SMEM)] + [pl.BlockSpec(memory_space=pltpu.VMEM)] * n


def final_kernel(
    in_ref, silu_ref, scale_ref, m_ref, cf_ref, cb_ref, gain_ref, w_ref, out_ref, normed_ref
):
    square = jnp.zeros((Q, 128), F32)
    for j in range(E // FW):
        at = pl.ds(FW * j, FW)
        y = in_ref[:, at].astype(F32)
        for d, c_ref in enumerate((cf_ref, cb_ref)):
            factor = dot(scale_ref[...], head_select(j, 4 * H, FW, 2 * H * d, 2))
            m = jnp.concatenate([m_ref[d, FW // 128 * j + k] for k in range(FW // 128)], axis=1)
            y = y + factor * dot(c_ref[...], m)
        gated = y * silu_ref[:, at].astype(F32)
        for k in range(FW // 128):
            part = gated[:, 128 * k : 128 * (k + 1)]
            square = square + part * part
        normed_ref[:, at] = (gated * gain_ref[:, at]).astype(BF16)
    mean = jnp.sum(square, axis=1, keepdims=True) * (1.0 / E)
    scale = lax.rsqrt(mean + 1e-05)
    for n in range(D // 256):
        at = pl.ds(256 * n, 256)
        out_ref[:, at] = (dot(normed_ref[...], w_ref[:, at]) * scale).astype(BF16)


def final_call(inside, silu, scale, m, c_f, c_b, gain, weight):
    return pl.pallas_call(
        final_kernel,
        in_specs=[pl.BlockSpec(memory_space=pltpu.VMEM)] * 8,
        out_specs=pl.BlockSpec(memory_space=pltpu.VMEM),
        out_shape=jax.ShapeDtypeStruct((Q, D), BF16),
        scratch_shapes=[pltpu.VMEM((Q, E), BF16)],
        compiler_params=LIMIT,
        name="gate_norm_project",
    )(inside, silu, scale, m, c_f, c_b, gain, weight)


def per_device(
    features, gate_input, b_forward, c_forward, b_backward, c_backward,
    rate_forward, rate_backward, norm_gain, out_weight,
):
    count, groups = lax.axis_size("seq"), lax.axis_size("grp")
    states, logs = state_call(features, rate_forward, rate_backward, b_forward, b_backward)
    states = states.reshape(count, N, 128)
    member, group = lax.axis_index("seq"), lax.axis_index("grp")
    backward = (member >= count // 2).astype(jnp.int32)
    mine = jnp.where(backward == 1, groups - 1 - group, group)
    place = jnp.stack([backward, mine, 2 * member]).astype(jnp.int32)
    parts = lax.all_to_all(states, "seq", 0, 0, tiled=True)
    logs = lax.all_gather(logs, "seq", tiled=True)
    keep = pltpu.VMEM((count, 128), F32)
    totals = pl.pallas_call(
        functools.partial(total_kernel, count, groups),
        in_specs=vmem_specs(2),
        out_specs=pl.BlockSpec(memory_space=pltpu.VMEM),
        out_shape=jax.ShapeDtypeStruct((groups, ROWS, 128), BF16),
        scratch_shapes=[keep],
        compiler_params=LIMIT,
        name="group_totals",
    )(place, logs, parts)
    totals = lax.all_to_all(totals, "grp", 0, 0, tiled=True)
    entries = pl.pallas_call(
        functools.partial(entry_kernel, count, groups),
        in_specs=vmem_specs(3),
        out_specs=pl.BlockSpec(memory_space=pltpu.VMEM),
        out_shape=jax.ShapeDtypeStruct((count, N, 128), BF16),
        scratch_shapes=[keep],
        compiler_params=LIMIT,
        name="entry_states",
    )(place, totals, logs, parts)
    m = lax.all_to_all(entries, "seq", 0, 0, tiled=True).reshape(2, E // 128, N, 128)
    inside, silu, scale = inside_call(
        features, gate_input, rate_forward, rate_backward,
        b_forward, c_forward, b_backward, c_backward, out_weight,
    )
    return final_call(
        inside, silu, scale, m, c_forward, c_backward, norm_gain.reshape(1, E), out_weight
    )


def solution(mesh):
    rows = P(("grp", "seq"), None)
    heads = P(None, ("grp", "seq"))
    placed = (rows,) * 6 + (heads, heads, P(), P())
    return jax.shard_map(per_device, mesh=mesh, in_specs=placed, out_specs=rows, check_vma=False)
```

```python
import functools
import jax
import jax.numpy as jnp
from jax import lax
from jax.experimental import pallas as pl
from jax.experimental.pallas import tpu as pltpu
from jax.sharding import PartitionSpec as P

Q = 256
H = 32
HEAD = 64
N = 128
E = 2048
D = 1024
BLK = 256
STEPS = E // BLK
FW = 256
FINAL_VMEM = 59400000
HPB = BLK // HEAD
ROWS = N + 16
LOG2E = 1.4426950408889634
F32 = jnp.float32
BF16 = jnp.bfloat16
LIMIT = pltpu.CompilerParams(vmem_limit_bytes=24 * 1024 * 1024)


def lane_sums(r):
    width = r.shape[1]
    lane = lax.broadcasted_iota(jnp.int32, r.shape, 1)
    shift = 1
    while shift < width:
        r = r + jnp.where(lane >= shift, pltpu.roll(r, shift, 1), 0.0)
        shift *= 2
    return r


def lane_sums_back(r):
    width = r.shape[1]
    lane = lax.broadcasted_iota(jnp.int32, r.shape, 1)
    shift = 1
    while shift < width:
        r = r + jnp.where(lane < width - shift, pltpu.roll(r, width - shift, 1), 0.0)
        shift *= 2
    return r


def step_of(r):
    y = 2.0 * r
    s = jnp.full_like(y, 1.0)
    for k in range(9, 1, -1):
        s = 1.0 - y * (1.0 / k) * s
    return jnp.sqrt(jnp.where(y < 0.5, y * s, 1.0 - jnp.exp(-y)))


def two_parts(a):
    high = a.astype(BF16).astype(F32)
    return high, a - high


def head_select(block, rows, width, first):
    row = lax.broadcasted_iota(jnp.int32, (rows, width), 0) - first
    column = lax.broadcasted_iota(jnp.int32, (rows, width), 1)
    head = block * (width // HEAD) + column // HEAD
    return jnp.where((row == head) | (row == head + H), 1.0, 0.0).astype(BF16)


def dot(a, b):
    return jnp.dot(a, b, preferred_element_type=F32)


def three_rows(value, width):
    high, rest = two_parts(value)
    middle, low = two_parts(rest)
    row = lax.broadcasted_iota(jnp.int32, (16, width), 0)
    tail = jnp.where(row == 0, high, jnp.where(row == 1, middle, jnp.where(row == 2, low, 0.0)))
    return tail.astype(BF16)


def state_kernel(
    x_hbm, rf_hbm, rb_hbm, bf_hbm, bb_hbm, out_ref, x_ref, r_ref, b_ref, select_ref, sems
):
    copies = [
        pltpu.make_async_copy(rf_hbm, r_ref.at[0], sems.at[0]),
        pltpu.make_async_copy(rb_hbm, r_ref.at[1], sems.at[1]),
        pltpu.make_async_copy(bf_hbm, b_ref.at[0], sems.at[2]),
        pltpu.make_async_copy(bb_hbm, b_ref.at[1], sems.at[3]),
        pltpu.make_async_copy(x_hbm, x_ref, sems.at[4]),
    ]
    for copy in copies:
        copy.start()
    select_ref[...] = head_select(0, 2 * H, E, 0)
    copies[0].wait()
    copies[1].wait()
    scales = []
    for d, sums in enumerate((lane_sums, lane_sums_back)):
        r = r_ref[d]
        c = sums(r)
        total = c[:, Q - 1 : Q] if d == 0 else c[:, 0:1]
        parts = two_parts(step_of(r) * jnp.exp(c - total))
        scales.append(jnp.concatenate(parts, axis=0).T.astype(BF16))
        keep = jnp.broadcast_to(jnp.exp(-total), (H, 128))
        lane = lax.broadcasted_iota(jnp.int32, (H, 128), 1)
        for k in range(E // 128):
            own = jnp.where(lane < HEAD, keep[2 * k : 2 * k + 1], keep[2 * k + 1 : 2 * k + 2])
            out_ref[d, k, N:ROWS, :] = three_rows(own[:1], 128)
    copies[2].wait()
    copies[3].wait()
    turned = [b_ref[d].astype(F32).T.astype(BF16) for d in range(2)]
    copies[4].wait()
    x = x_ref[...].astype(F32)
    for d in range(2):
        factor = dot(scales[d], select_ref[...])
        s = dot(turned[d], (x * factor).astype(BF16)).astype(BF16)
        for k in range(E // 128):
            out_ref[d, k, 0:N, :] = s[:, 128 * k : 128 * (k + 1)]


def state_call(x, rate_f, rate_b, b_f, b_b):
    return pl.pallas_call(
        state_kernel,
        in_specs=[pl.BlockSpec(memory_space=pltpu.HBM)] * 5,
        out_specs=pl.BlockSpec(memory_space=pltpu.VMEM),
        out_shape=jax.ShapeDtypeStruct((2, E // 128, ROWS, 128), BF16),
        scratch_shapes=[
            pltpu.VMEM((Q, E), BF16),
            pltpu.VMEM((2, H, Q), F32),
            pltpu.VMEM((2, Q, N), BF16),
            pltpu.VMEM((2 * H, E), BF16),
            pltpu.SemaphoreType.DMA((5,)),
        ],
        compiler_params=pltpu.CompilerParams(vmem_limit_bytes=60 * 1024 * 1024),
        name="span_states",
    )(x, rate_f, rate_b, b_f, b_b)


def inside_kernel(
    x_ref, gate_ref, rf_ref, rb_ref, bf_ref, cf_ref, bb_ref, cb_ref,
    out_ref, silu_ref, scale_ref, score_ref, rows_ref, cols_ref,
):
    j = pl.program_id(0)
    t = lax.broadcasted_iota(jnp.int32, (Q, Q), 0)
    s = lax.broadcasted_iota(jnp.int32, (Q, Q), 1)

    @pl.when(j == 0)
    def _():
        contract = (((1,), (1,)), ((), ()))
        forward = lax.dot_general(cf_ref[...], bf_ref[...], contract, preferred_element_type=F32)
        backward = lax.dot_general(cb_ref[...], bb_ref[...], contract, preferred_element_type=F32)
        score_ref[...] = jnp.where(s <= t, forward, backward)
        own = jnp.sum(jnp.where(s == t, backward, 0.0), axis=0, keepdims=True)
        c_f = lane_sums(rf_ref[...]) * LOG2E
        c_b = lane_sums_back(rb_ref[...]) * LOG2E
        step_f = step_of(rf_ref[...])
        step_b = step_of(rb_ref[...])
        rows_ref[0] = c_f + jnp.log(step_f) * LOG2E
        rows_ref[1] = c_b + jnp.log(step_b) * LOG2E
        high, low = two_parts(own * step_b)
        cols_ref[...] = jnp.concatenate([c_f, c_b, high, low], axis=0).T
        parts = two_parts(jnp.exp2(-c_f)) + two_parts(jnp.exp2(-c_b))
        scale_ref[...] = jnp.concatenate(parts, axis=0).T.astype(BF16)

    gate = gate_ref[...].astype(F32)
    silu_ref[...] = (gate * jax.nn.sigmoid(gate)).astype(BF16)
    cols = cols_ref[...]
    own = dot(cols.astype(BF16), head_select(j, 4 * H, BLK, 2 * H))
    cols = pltpu.roll(cols, lax.rem(4 * H - HPB * j, 4 * H), 1)
    lane = lax.broadcasted_iota(jnp.int32, (Q, 128), 1)
    for p in range(HPB // 2):
        x = x_ref[:, 128 * p : 128 * (p + 1)]
        halves = []
        for i in (2 * p, 2 * p + 1):
            forward = rows_ref[0, pl.ds(HPB * j + i, 1), :] - cols[:, i : i + 1]
            backward = rows_ref[1, pl.ds(HPB * j + i, 1), :] - cols[:, H + i : H + i + 1]
            w = score_ref[...] * jnp.exp2(jnp.where(s <= t, forward, backward))
            halves.append(dot(w.astype(BF16), x))
        y = jnp.where(lane < HEAD, halves[0], halves[1])
        y = y + own[:, 128 * p : 128 * (p + 1)] * x.astype(F32)
        out_ref[:, 128 * p : 128 * (p + 1)] = y.astype(BF16)


def inside_call(x, gate, rate_f, rate_b, b_f, c_f, b_b, c_b):
    whole = lambda shape: pl.BlockSpec(shape, lambda j: (0,) * len(shape))
    columns = pl.BlockSpec((Q, BLK), lambda j: (0, j))
    return pl.pallas_call(
        inside_kernel,
        grid=(STEPS,),
        in_specs=[columns, columns, whole((H, Q)), whole((H, Q))] + [whole((Q, N))] * 4,
        out_specs=[columns, columns, whole((Q, 4 * H))],
        out_shape=[jax.ShapeDtypeStruct((Q, E), BF16)] * 2
        + [jax.ShapeDtypeStruct((Q, 4 * H), BF16)],
        compiler_params=LIMIT,
        scratch_shapes=[
            pltpu.VMEM((Q, Q), F32),
            pltpu.VMEM((2, H, Q), F32),
            pltpu.VMEM((Q, 4 * H), F32),
        ],
        cost_estimate=pl.CostEstimate(
            flops=2 * H * Q * Q * 128, bytes_accessed=4 * Q * E * 2, transcendentals=H * Q * Q
        ),
        name="inside_spans",
    )(x, gate, rate_f, rate_b, b_f, c_f, b_b, c_b)


def read_part(ref, index):
    state = ref[index, 0:N, :].astype(F32)
    tail = ref[index, N:ROWS, :].astype(F32)
    return state, tail[0:1] + tail[1:2] + tail[2:3]


def total_kernel(count, copies, place_ref, parts_ref, out_ref):
    backward = place_ref[0]

    def step(i, carried):
        state, kept = carried
        index = jnp.where(backward == 1, count - 1 - i, i)
        own, keep = read_part(parts_ref, index)
        return keep * state + own, keep * kept

    state, kept = lax.fori_loop(
        0, count, step, (jnp.zeros((N, 128), F32), jnp.ones((1, 128), F32)), unroll=4
    )
    tail = three_rows(kept, 128)
    for g in range(copies):
        out_ref[g, 0:N, :] = state.astype(BF16)
        out_ref[g, N:ROWS, :] = tail


def entry_kernel(count, groups, place_ref, totals_ref, parts_ref, out_ref):
    backward, mine = place_ref[0], place_ref[1]

    def outer(i, state):
        index = jnp.where(backward == 1, groups - 1 - i, i)
        own, keep = read_part(totals_ref, index)
        return keep * state + own

    state = lax.fori_loop(0, mine, outer, jnp.zeros((N, 128), F32))

    def step(i, state):
        index = jnp.where(backward == 1, count - 1 - i, i)
        out_ref[index] = state.astype(BF16)
        own, keep = read_part(parts_ref, index)
        return keep * state + own

    lax.fori_loop(0, count, step, state, unroll=4)


def vmem_specs(n):
    return [pl.BlockSpec(memory_space=pltpu.SMEM)] + [pl.BlockSpec(memory_space=pltpu.VMEM)] * n


def final_kernel(
    in_ref, silu_ref, scale_ref, m_ref, cf_ref, cb_ref, gain_ref, w_hbm,
    out_ref, normed_ref, w_ref, sem,
):
    copy = pltpu.make_async_copy(w_hbm, w_ref, sem)
    copy.start()
    scales = [scale_ref[:, 2 * H * d : 2 * H * (d + 1)] for d in range(2)]
    square = jnp.zeros((Q, 128), F32)
    for j in range(E // FW):
        at = pl.ds(FW * j, FW)
        y = in_ref[:, at].astype(F32)
        select = head_select(j, 2 * H, FW, 0)
        for d, c_ref in enumerate((cf_ref, cb_ref)):
            m = jnp.concatenate([m_ref[d, FW // 128 * j + k] for k in range(FW // 128)], axis=1)
            y = y + dot(scales[d], select) * dot(c_ref[...], m)
        gated = y * silu_ref[:, at].astype(F32)
        for k in range(FW // 128):
            part = gated[:, 128 * k : 128 * (k + 1)]
            square = square + part * part
        normed_ref[:, at] = (gated * gain_ref[:, at]).astype(BF16)
    mean = jnp.sum(square, axis=1, keepdims=True) * (1.0 / E)
    scale = lax.rsqrt(mean + 1e-05)
    copy.wait()
    for n in range(D // 256):
        at = pl.ds(256 * n, 256)
        out_ref[:, at] = (dot(normed_ref[...], w_ref[:, at]) * scale).astype(BF16)


def final_call(inside, silu, scale, m, c_f, c_b, gain, weight):
    return pl.pallas_call(
        final_kernel,
        in_specs=[pl.BlockSpec(memory_space=pltpu.VMEM)] * 7
        + [pl.BlockSpec(memory_space=pltpu.HBM)],
        out_specs=pl.BlockSpec(memory_space=pltpu.VMEM),
        out_shape=jax.ShapeDtypeStruct((Q, D), BF16),
        scratch_shapes=[
            pltpu.VMEM((Q, E), BF16),
            pltpu.VMEM((E, D), BF16),
            pltpu.SemaphoreType.DMA,
        ],
        compiler_params=pltpu.CompilerParams(vmem_limit_bytes=FINAL_VMEM),
        name="gate_norm_project",
    )(inside, silu, scale, m, c_f, c_b, gain, weight)


def per_device(
    features, gate_input, b_forward, c_forward, b_backward, c_backward,
    rate_forward, rate_backward, norm_gain, out_weight,
):
    count, groups = lax.axis_size("seq"), lax.axis_size("grp")
    states = state_call(features, rate_forward, rate_backward, b_forward, b_backward)
    states = states.reshape(count, ROWS, 128)
    backward = (lax.axis_index("seq") >= count // 2).astype(jnp.int32)
    group = lax.axis_index("grp")
    mine = jnp.where(backward == 1, groups - 1 - group, group)
    place = jnp.stack([backward, mine]).astype(jnp.int32)
    parts = lax.all_to_all(states, "seq", 0, 0, tiled=True)
    totals = pl.pallas_call(
        functools.partial(total_kernel, count, groups),
        in_specs=vmem_specs(1),
        out_specs=pl.BlockSpec(memory_space=pltpu.VMEM),
        out_shape=jax.ShapeDtypeStruct((groups, ROWS, 128), BF16),
        compiler_params=LIMIT,
        name="group_totals",
    )(place, parts)
    totals = lax.all_to_all(totals, "grp", 0, 0, tiled=True)
    entries = pl.pallas_call(
        functools.partial(entry_kernel, count, groups),
        in_specs=vmem_specs(2),
        out_specs=pl.BlockSpec(memory_space=pltpu.VMEM),
        out_shape=jax.ShapeDtypeStruct((count, N, 128), BF16),
        compiler_params=LIMIT,
        name="entry_states",
    )(place, totals, parts)
    m = lax.all_to_all(entries, "seq", 0, 0, tiled=True).reshape(2, E // 128, N, 128)
    inside, silu, scale = inside_call(
        features, gate_input, rate_forward, rate_backward,
        b_forward, c_forward, b_backward, c_backward,
    )
    return final_call(
        inside, silu, scale, m, c_forward, c_backward, norm_gain.reshape(1, E), out_weight
    )


def solution(mesh):
    rows = P(("grp", "seq"), None)
    heads = P(None, ("grp", "seq"))
    placed = (rows,) * 6 + (heads, heads, P(), P())
    return jax.shard_map(per_device, mesh=mesh, in_specs=placed, out_specs=rows, check_vma=False)
```

```python
import functools
import jax
import jax.numpy as jnp
from jax import lax
from jax.experimental import pallas as pl
from jax.experimental.pallas import tpu as pltpu
from jax.sharding import PartitionSpec as P

Q = 256
H = 32
HEAD = 64
N = 128
E = 2048
D = 1024
BLK = 256
STEPS = E // BLK
FW = 256
FINAL_VMEM = 48 * 1024 * 1024
HPB = BLK // HEAD
ROWS = N + 16
CHUNKS = 4
LOG2E = 1.4426950408889634
F32 = jnp.float32
BF16 = jnp.bfloat16
LIMIT = pltpu.CompilerParams(vmem_limit_bytes=24 * 1024 * 1024)


def lane_sums(r):
    width = r.shape[1]
    lane = lax.broadcasted_iota(jnp.int32, r.shape, 1)
    shift = 1
    while shift < width:
        r = r + jnp.where(lane >= shift, pltpu.roll(r, shift, 1), 0.0)
        shift *= 2
    return r


def lane_sums_back(r):
    width = r.shape[1]
    lane = lax.broadcasted_iota(jnp.int32, r.shape, 1)
    shift = 1
    while shift < width:
        r = r + jnp.where(lane < width - shift, pltpu.roll(r, width - shift, 1), 0.0)
        shift *= 2
    return r


def step_of(r):
    y = 2.0 * r
    s = jnp.full_like(y, 1.0)
    for k in range(9, 1, -1):
        s = 1.0 - y * (1.0 / k) * s
    return jnp.sqrt(jnp.where(y < 0.5, y * s, 1.0 - jnp.exp(-y)))


def two_parts(a):
    high = a.astype(BF16).astype(F32)
    return high, a - high


def head_select(block, rows, width, first):
    row = lax.broadcasted_iota(jnp.int32, (rows, width), 0) - first
    column = lax.broadcasted_iota(jnp.int32, (rows, width), 1)
    head = block * (width // HEAD) + column // HEAD
    return jnp.where((row == head) | (row == head + H), 1.0, 0.0).astype(BF16)


def dot(a, b):
    return jnp.dot(a, b, preferred_element_type=F32)


def three_rows(value, width):
    high, rest = two_parts(value)
    middle, low = two_parts(rest)
    row = lax.broadcasted_iota(jnp.int32, (16, width), 0)
    tail = jnp.where(row == 0, high, jnp.where(row == 1, middle, jnp.where(row == 2, low, 0.0)))
    return tail.astype(BF16)


def state_kernel(
    x_hbm, rf_hbm, rb_hbm, bf_hbm, bb_hbm, out_hbm,
    x_ref, r_ref, b_ref, select_ref, out_ref, sems,
):
    copies = [
        pltpu.make_async_copy(rf_hbm, r_ref.at[0], sems.at[0]),
        pltpu.make_async_copy(rb_hbm, r_ref.at[1], sems.at[1]),
        pltpu.make_async_copy(bf_hbm, b_ref.at[0], sems.at[2]),
        pltpu.make_async_copy(bb_hbm, b_ref.at[1], sems.at[3]),
        pltpu.make_async_copy(x_hbm, x_ref, sems.at[4]),
    ]
    for copy in copies:
        copy.start()
    select_ref[...] = head_select(0, 2 * H, E, 0)
    copies[0].wait()
    copies[1].wait()
    scales = []
    for d, sums in enumerate((lane_sums, lane_sums_back)):
        r = r_ref[d]
        c = sums(r)
        total = c[:, Q - 1 : Q] if d == 0 else c[:, 0:1]
        parts = two_parts(step_of(r) * jnp.exp(c - total))
        scales.append(jnp.concatenate(parts, axis=0).T.astype(BF16))
        keep = jnp.broadcast_to(jnp.exp(-total), (H, 128))
        lane = lax.broadcasted_iota(jnp.int32, (H, 128), 1)
        for k in range(E // 128):
            own = jnp.where(lane < HEAD, keep[2 * k : 2 * k + 1], keep[2 * k + 1 : 2 * k + 2])
            out_ref[d, k, N:ROWS, :] = three_rows(own[:1], 128)
    copies[2].wait()
    copies[3].wait()
    turned = [b_ref[d].astype(F32).T.astype(BF16) for d in range(2)]
    copies[4].wait()
    x = x_ref[...].astype(F32)
    for d in range(2):
        factor = dot(scales[d], select_ref[...])
        s = dot(turned[d], (x * factor).astype(BF16)).astype(BF16)
        for k in range(E // 128):
            out_ref[d, k, 0:N, :] = s[:, 128 * k : 128 * (k + 1)]
        copies.append(pltpu.make_async_copy(out_ref.at[d], out_hbm.at[d], sems.at[5 + d]))
        copies[-1].start()
    copies[5].wait()
    copies[6].wait()


def state_call(x, rate_f, rate_b, b_f, b_b):
    return pl.pallas_call(
        state_kernel,
        in_specs=[pl.BlockSpec(memory_space=pltpu.HBM)] * 5,
        out_specs=pl.BlockSpec(memory_space=pltpu.HBM),
        out_shape=jax.ShapeDtypeStruct((2, E // 128, ROWS, 128), BF16),
        scratch_shapes=[
            pltpu.VMEM((Q, E), BF16),
            pltpu.VMEM((2, H, Q), F32),
            pltpu.VMEM((2, Q, N), BF16),
            pltpu.VMEM((2 * H, E), BF16),
            pltpu.VMEM((2, E // 128, ROWS, 128), BF16),
            pltpu.SemaphoreType.DMA((7,)),
        ],
        compiler_params=pltpu.CompilerParams(vmem_limit_bytes=60 * 1024 * 1024),
        name="span_states",
    )(x, rate_f, rate_b, b_f, b_b)


def inside_kernel(
    x_ref, gate_ref, rf_ref, rb_ref, bf_ref, cf_ref, bb_ref, cb_ref,
    out_ref, silu_ref, scale_ref, score_ref, rows_ref, cols_ref,
):
    j = pl.program_id(0)
    t = lax.broadcasted_iota(jnp.int32, (Q, Q), 0)
    s = lax.broadcasted_iota(jnp.int32, (Q, Q), 1)

    @pl.when(j == 0)
    def _():
        contract = (((1,), (1,)), ((), ()))
        forward = lax.dot_general(cf_ref[...], bf_ref[...], contract, preferred_element_type=F32)
        backward = lax.dot_general(cb_ref[...], bb_ref[...], contract, preferred_element_type=F32)
        score_ref[...] = jnp.where(s <= t, forward, backward)
        own = jnp.sum(jnp.where(s == t, backward, 0.0), axis=0, keepdims=True)
        c_f = lane_sums(rf_ref[...]) * LOG2E
        c_b = lane_sums_back(rb_ref[...]) * LOG2E
        step_f = step_of(rf_ref[...])
        step_b = step_of(rb_ref[...])
        rows_ref[0] = c_f + jnp.log(step_f) * LOG2E
        rows_ref[1] = c_b + jnp.log(step_b) * LOG2E
        high, low = two_parts(own * step_b)
        cols_ref[...] = jnp.concatenate([c_f, c_b, high, low], axis=0).T
        parts = two_parts(jnp.exp2(-c_f)) + two_parts(jnp.exp2(-c_b))
        scale_ref[...] = jnp.concatenate(parts, axis=0).T.astype(BF16)

    gate = gate_ref[...].astype(F32)
    silu_ref[...] = (gate * jax.nn.sigmoid(gate)).astype(BF16)
    cols = cols_ref[...]
    own = dot(cols.astype(BF16), head_select(j, 4 * H, BLK, 2 * H))
    cols = pltpu.roll(cols, lax.rem(4 * H - HPB * j, 4 * H), 1)
    lane = lax.broadcasted_iota(jnp.int32, (Q, 128), 1)
    for p in range(HPB // 2):
        x = x_ref[:, 128 * p : 128 * (p + 1)]
        halves = []
        for i in (2 * p, 2 * p + 1):
            forward = rows_ref[0, pl.ds(HPB * j + i, 1), :] - cols[:, i : i + 1]
            backward = rows_ref[1, pl.ds(HPB * j + i, 1), :] - cols[:, H + i : H + i + 1]
            w = score_ref[...] * jnp.exp2(jnp.where(s <= t, forward, backward))
            halves.append(dot(w.astype(BF16), x))
        y = jnp.where(lane < HEAD, halves[0], halves[1])
        y = y + own[:, 128 * p : 128 * (p + 1)] * x.astype(F32)
        out_ref[:, 128 * p : 128 * (p + 1)] = y.astype(BF16)


def inside_call(x, gate, rate_f, rate_b, b_f, c_f, b_b, c_b):
    whole = lambda shape: pl.BlockSpec(shape, lambda j: (0,) * len(shape))
    columns = pl.BlockSpec((Q, BLK), lambda j: (0, j))
    return pl.pallas_call(
        inside_kernel,
        grid=(STEPS,),
        in_specs=[columns, columns, whole((H, Q)), whole((H, Q))] + [whole((Q, N))] * 4,
        out_specs=[columns, columns, whole((Q, 4 * H))],
        out_shape=[jax.ShapeDtypeStruct((Q, E), BF16)] * 2
        + [jax.ShapeDtypeStruct((Q, 4 * H), BF16)],
        compiler_params=LIMIT,
        scratch_shapes=[
            pltpu.VMEM((Q, Q), F32),
            pltpu.VMEM((2, H, Q), F32),
            pltpu.VMEM((Q, 4 * H), F32),
        ],
        cost_estimate=pl.CostEstimate(
            flops=2 * H * Q * Q * 128, bytes_accessed=4 * Q * E * 2, transcendentals=H * Q * Q
        ),
        name="inside_spans",
    )(x, gate, rate_f, rate_b, b_f, c_f, b_b, c_b)


def read_part(ref, index):
    state = ref[index, 0:N, :].astype(F32)
    tail = ref[index, N:ROWS, :].astype(F32)
    return state, tail[0:1] + tail[1:2] + tail[2:3]


def total_kernel(count, copies, place_ref, parts_ref, out_ref):
    backward = place_ref[0]

    def step(i, carried):
        state, kept = carried
        index = jnp.where(backward == 1, count - 1 - i, i)
        own, keep = read_part(parts_ref, index)
        return keep * state + own, keep * kept

    state, kept = lax.fori_loop(
        0, count, step, (jnp.zeros((N, 128), F32), jnp.ones((1, 128), F32)), unroll=4
    )
    tail = three_rows(kept, 128)
    for g in range(copies):
        out_ref[g, 0:N, :] = state.astype(BF16)
        out_ref[g, N:ROWS, :] = tail


def entry_kernel(count, groups, place_ref, totals_ref, parts_ref, out_hbm, out_ref, sems):
    backward, mine = place_ref[0], place_ref[1]

    def outer(i, state):
        index = jnp.where(backward == 1, groups - 1 - i, i)
        own, keep = read_part(totals_ref, index)
        return keep * state + own

    state = lax.fori_loop(0, mine, outer, jnp.zeros((N, 128), F32))
    chunk = count // CHUNKS
    copies = []
    for q in range(CHUNKS):
        first = jnp.where(backward == 1, count - chunk * (q + 1), chunk * q)
        for i in range(chunk):
            index = first + jnp.where(backward == 1, chunk - 1 - i, i)
            out_ref[index] = state.astype(BF16)
            own, keep = read_part(parts_ref, index)
            state = keep * state + own
        span = pl.ds(first, chunk)
        copies.append(pltpu.make_async_copy(out_ref.at[span], out_hbm.at[span], sems.at[q]))
        copies[-1].start()
    for copy in copies:
        copy.wait()


def vmem_specs(n):
    return [pl.BlockSpec(memory_space=pltpu.SMEM)] + [pl.BlockSpec(memory_space=pltpu.VMEM)] * n


def final_kernel(
    in_ref, silu_ref, scale_ref, m_ref, cf_ref, cb_ref, gain_ref, w_hbm,
    out_hbm, normed_ref, w_ref, out_ref, sems,
):
    copies = [pltpu.make_async_copy(w_hbm, w_ref, sems.at[0])]
    copies[0].start()
    scales = [scale_ref[:, 2 * H * d : 2 * H * (d + 1)] for d in range(2)]
    square = jnp.zeros((Q, 128), F32)
    for j in range(E // FW):
        at = pl.ds(FW * j, FW)
        y = in_ref[:, at].astype(F32)
        select = head_select(j, 2 * H, FW, 0)
        for d, c_ref in enumerate((cf_ref, cb_ref)):
            m = jnp.concatenate([m_ref[d, FW // 128 * j + k] for k in range(FW // 128)], axis=1)
            y = y + dot(scales[d], select) * dot(c_ref[...], m)
        gated = y * silu_ref[:, at].astype(F32)
        for k in range(FW // 128):
            part = gated[:, 128 * k : 128 * (k + 1)]
            square = square + part * part
        normed_ref[:, at] = (gated * gain_ref[:, at]).astype(BF16)
    mean = jnp.sum(square, axis=1, keepdims=True) * (1.0 / E)
    scale = lax.rsqrt(mean + 1e-05)
    copies[0].wait()
    half = Q // 2
    for n in range(2):
        rows = pl.ds(half * n, half)
        mixed = dot(normed_ref[rows, :], w_ref[...]) * scale[half * n : half * (n + 1)]
        out_ref[rows, :] = mixed.astype(BF16)
        copies.append(pltpu.make_async_copy(out_ref.at[rows], out_hbm.at[rows], sems.at[n + 1]))
        copies[-1].start()
    copies[1].wait()
    copies[2].wait()


def final_call(inside, silu, scale, m, c_f, c_b, gain, weight):
    return pl.pallas_call(
        final_kernel,
        in_specs=[pl.BlockSpec(memory_space=pltpu.VMEM)] * 7
        + [pl.BlockSpec(memory_space=pltpu.HBM)],
        out_specs=pl.BlockSpec(memory_space=pltpu.HBM),
        out_shape=jax.ShapeDtypeStruct((Q, D), BF16),
        scratch_shapes=[
            pltpu.VMEM((Q, E), BF16),
            pltpu.VMEM((E, D), BF16),
            pltpu.VMEM((Q, D), BF16),
            pltpu.SemaphoreType.DMA((3,)),
        ],
        compiler_params=pltpu.CompilerParams(vmem_limit_bytes=FINAL_VMEM),
        name="gate_norm_project",
    )(inside, silu, scale, m, c_f, c_b, gain, weight)


def per_device(
    features, gate_input, b_forward, c_forward, b_backward, c_backward,
    rate_forward, rate_backward, norm_gain, out_weight,
):
    count, groups = lax.axis_size("seq"), lax.axis_size("grp")
    states = state_call(features, rate_forward, rate_backward, b_forward, b_backward)
    states = states.reshape(count, ROWS, 128)
    backward = (lax.axis_index("seq") >= count // 2).astype(jnp.int32)
    group = lax.axis_index("grp")
    mine = jnp.where(backward == 1, groups - 1 - group, group)
    place = jnp.stack([backward, mine]).astype(jnp.int32)
    parts = lax.all_to_all(states, "seq", 0, 0, tiled=True)
    totals = pl.pallas_call(
        functools.partial(total_kernel, count, groups),
        in_specs=vmem_specs(1),
        out_specs=pl.BlockSpec(memory_space=pltpu.VMEM),
        out_shape=jax.ShapeDtypeStruct((groups, ROWS, 128), BF16),
        compiler_params=LIMIT,
        name="group_totals",
    )(place, parts)
    totals = lax.all_to_all(totals, "grp", 0, 0, tiled=True)
    entries = pl.pallas_call(
        functools.partial(entry_kernel, count, groups),
        in_specs=vmem_specs(2),
        out_specs=pl.BlockSpec(memory_space=pltpu.HBM),
        out_shape=jax.ShapeDtypeStruct((count, N, 128), BF16),
        scratch_shapes=[
            pltpu.VMEM((count, N, 128), BF16),
            pltpu.SemaphoreType.DMA((CHUNKS,)),
        ],
        compiler_params=LIMIT,
        name="entry_states",
    )(place, totals, parts)
    m = lax.all_to_all(entries, "seq", 0, 0, tiled=True).reshape(2, E // 128, N, 128)
    inside, silu, scale = inside_call(
        features, gate_input, rate_forward, rate_backward,
        b_forward, c_forward, b_backward, c_backward,
    )
    return final_call(
        inside, silu, scale, m, c_forward, c_backward, norm_gain.reshape(1, E), out_weight
    )


def solution(mesh):
    rows = P(("grp", "seq"), None)
    heads = P(None, ("grp", "seq"))
    placed = (rows,) * 6 + (heads, heads, P(), P())
    return jax.shard_map(per_device, mesh=mesh, in_specs=placed, out_specs=rows, check_vma=False)
```

```python
import functools
import jax
import jax.numpy as jnp
from jax import lax
from jax.experimental import pallas as pl
from jax.experimental.pallas import tpu as pltpu
from jax.sharding import PartitionSpec as P

Q = 256
H = 32
HEAD = 64
N = 128
E = 2048
D = 1024
BLK = 256
STEPS = E // BLK
FW = 256
FINAL_VMEM = 48 * 1024 * 1024
HPB = BLK // HEAD
ROWS = N + 16
CHUNKS = 4
YSIZE = 4
ZSIZE = 8
LOG2E = 1.4426950408889634
F32 = jnp.float32
BF16 = jnp.bfloat16
LIMIT = pltpu.CompilerParams(vmem_limit_bytes=24 * 1024 * 1024)


def lane_sums(r):
    width = r.shape[1]
    lane = lax.broadcasted_iota(jnp.int32, r.shape, 1)
    shift = 1
    while shift < width:
        r = r + jnp.where(lane >= shift, pltpu.roll(r, shift, 1), 0.0)
        shift *= 2
    return r


def lane_sums_back(r):
    width = r.shape[1]
    lane = lax.broadcasted_iota(jnp.int32, r.shape, 1)
    shift = 1
    while shift < width:
        r = r + jnp.where(lane < width - shift, pltpu.roll(r, width - shift, 1), 0.0)
        shift *= 2
    return r


def step_of(r):
    y = 2.0 * r
    s = jnp.full_like(y, 1.0)
    for k in range(9, 1, -1):
        s = 1.0 - y * (1.0 / k) * s
    return jnp.sqrt(jnp.where(y < 0.5, y * s, 1.0 - jnp.exp(-y)))


def two_parts(a):
    high = a.astype(BF16).astype(F32)
    return high, a - high


def head_select(block, rows, width, first):
    row = lax.broadcasted_iota(jnp.int32, (rows, width), 0) - first
    column = lax.broadcasted_iota(jnp.int32, (rows, width), 1)
    head = block * (width // HEAD) + column // HEAD
    return jnp.where((row == head) | (row == head + H), 1.0, 0.0).astype(BF16)


def dot(a, b):
    return jnp.dot(a, b, preferred_element_type=F32)


def three_rows(value, width):
    high, rest = two_parts(value)
    middle, low = two_parts(rest)
    row = lax.broadcasted_iota(jnp.int32, (16, width), 0)
    tail = jnp.where(row == 0, high, jnp.where(row == 1, middle, jnp.where(row == 2, low, 0.0)))
    return tail.astype(BF16)


def state_kernel(
    x_hbm, rf_hbm, rb_hbm, bf_hbm, bb_hbm, out_hbm, total_ref,
    x_ref, r_ref, b_ref, select_ref, out_ref, sems,
):
    copies = [
        pltpu.make_async_copy(rf_hbm, r_ref.at[0], sems.at[0]),
        pltpu.make_async_copy(rb_hbm, r_ref.at[1], sems.at[1]),
        pltpu.make_async_copy(bf_hbm, b_ref.at[0], sems.at[2]),
        pltpu.make_async_copy(bb_hbm, b_ref.at[1], sems.at[3]),
        pltpu.make_async_copy(x_hbm, x_ref, sems.at[4]),
    ]
    for copy in copies:
        copy.start()
    select_ref[...] = head_select(0, 2 * H, E, 0)
    copies[0].wait()
    copies[1].wait()
    scales, totals = [], 0.0
    for d, sums in enumerate((lane_sums, lane_sums_back)):
        r = r_ref[d]
        c = sums(r)
        total = c[:, Q - 1 : Q] if d == 0 else c[:, 0:1]
        parts = two_parts(step_of(r) * jnp.exp(c - total))
        scales.append(jnp.concatenate(parts, axis=0).T.astype(BF16))
        row = lax.broadcasted_iota(jnp.int32, (H, 128), 0)
        lane = lax.broadcasted_iota(jnp.int32, (H, 128), 1)
        totals = totals + jnp.where(lane == row + H * d, total, 0.0)
    total_ref[...] = jnp.sum(totals, axis=0, keepdims=True)
    copies[2].wait()
    copies[3].wait()
    turned = [b_ref[d].astype(F32).T.astype(BF16) for d in range(2)]
    copies[4].wait()
    x = x_ref[...].astype(F32)
    for d in range(2):
        factor = dot(scales[d], select_ref[...])
        s = dot(turned[d], (x * factor).astype(BF16)).astype(BF16)
        for k in range(E // 128):
            out_ref[d, k] = s[:, 128 * k : 128 * (k + 1)]
        copies.append(pltpu.make_async_copy(out_ref.at[d], out_hbm.at[d], sems.at[5 + d]))
        copies[-1].start()
    copies[5].wait()
    copies[6].wait()


def state_call(x, rate_f, rate_b, b_f, b_b):
    return pl.pallas_call(
        state_kernel,
        in_specs=[pl.BlockSpec(memory_space=pltpu.HBM)] * 5,
        out_specs=[pl.BlockSpec(memory_space=pltpu.HBM), pl.BlockSpec(memory_space=pltpu.VMEM)],
        out_shape=[
            jax.ShapeDtypeStruct((2, E // 128, N, 128), BF16),
            jax.ShapeDtypeStruct((1, 128), F32),
        ],
        scratch_shapes=[
            pltpu.VMEM((Q, E), BF16),
            pltpu.VMEM((2, H, Q), F32),
            pltpu.VMEM((2, Q, N), BF16),
            pltpu.VMEM((2 * H, E), BF16),
            pltpu.VMEM((2, E // 128, N, 128), BF16),
            pltpu.SemaphoreType.DMA((7,)),
        ],
        compiler_params=pltpu.CompilerParams(vmem_limit_bytes=60 * 1024 * 1024),
        name="span_states",
    )(x, rate_f, rate_b, b_f, b_b)


def inside_kernel(
    x_ref, gate_ref, rf_ref, rb_ref, bf_ref, cf_ref, bb_ref, cb_ref,
    out_ref, silu_ref, scale_ref, score_ref, rows_ref, cols_ref,
):
    j = pl.program_id(0)
    t = lax.broadcasted_iota(jnp.int32, (Q, Q), 0)
    s = lax.broadcasted_iota(jnp.int32, (Q, Q), 1)

    @pl.when(j == 0)
    def _():
        contract = (((1,), (1,)), ((), ()))
        forward = lax.dot_general(cf_ref[...], bf_ref[...], contract, preferred_element_type=F32)
        backward = lax.dot_general(cb_ref[...], bb_ref[...], contract, preferred_element_type=F32)
        score_ref[...] = jnp.where(s <= t, forward, backward)
        own = jnp.sum(jnp.where(s == t, backward, 0.0), axis=0, keepdims=True)
        c_f = lane_sums(rf_ref[...]) * LOG2E
        c_b = lane_sums_back(rb_ref[...]) * LOG2E
        step_f = step_of(rf_ref[...])
        step_b = step_of(rb_ref[...])
        rows_ref[0] = c_f + jnp.log(step_f) * LOG2E
        rows_ref[1] = c_b + jnp.log(step_b) * LOG2E
        high, low = two_parts(own * step_b)
        cols_ref[...] = jnp.concatenate([c_f, c_b, high, low], axis=0).T
        parts = two_parts(jnp.exp2(-c_f)) + two_parts(jnp.exp2(-c_b))
        scale_ref[...] = jnp.concatenate(parts, axis=0).T.astype(BF16)

    gate = gate_ref[...].astype(F32)
    silu_ref[...] = (gate * jax.nn.sigmoid(gate)).astype(BF16)
    cols = cols_ref[...]
    own = dot(cols.astype(BF16), head_select(j, 4 * H, BLK, 2 * H))
    cols = pltpu.roll(cols, lax.rem(4 * H - HPB * j, 4 * H), 1)
    lane = lax.broadcasted_iota(jnp.int32, (Q, 128), 1)
    for p in range(HPB // 2):
        x = x_ref[:, 128 * p : 128 * (p + 1)]
        halves = []
        for i in (2 * p, 2 * p + 1):
            forward = rows_ref[0, pl.ds(HPB * j + i, 1), :] - cols[:, i : i + 1]
            backward = rows_ref[1, pl.ds(HPB * j + i, 1), :] - cols[:, H + i : H + i + 1]
            w = score_ref[...] * jnp.exp2(jnp.where(s <= t, forward, backward))
            halves.append(dot(w.astype(BF16), x))
        y = jnp.where(lane < HEAD, halves[0], halves[1])
        y = y + own[:, 128 * p : 128 * (p + 1)] * x.astype(F32)
        out_ref[:, 128 * p : 128 * (p + 1)] = y.astype(BF16)


def inside_call(x, gate, rate_f, rate_b, b_f, c_f, b_b, c_b):
    whole = lambda shape: pl.BlockSpec(shape, lambda j: (0,) * len(shape))
    columns = pl.BlockSpec((Q, BLK), lambda j: (0, j))
    return pl.pallas_call(
        inside_kernel,
        grid=(STEPS,),
        in_specs=[columns, columns, whole((H, Q)), whole((H, Q))] + [whole((Q, N))] * 4,
        out_specs=[columns, columns, whole((Q, 4 * H))],
        out_shape=[jax.ShapeDtypeStruct((Q, E), BF16)] * 2
        + [jax.ShapeDtypeStruct((Q, 4 * H), BF16)],
        compiler_params=LIMIT,
        scratch_shapes=[
            pltpu.VMEM((Q, Q), F32),
            pltpu.VMEM((2, H, Q), F32),
            pltpu.VMEM((Q, 4 * H), F32),
        ],
        cost_estimate=pl.CostEstimate(
            flops=2 * H * Q * Q * 128, bytes_accessed=4 * Q * E * 2, transcendentals=H * Q * Q
        ),
        name="inside_spans",
    )(x, gate, rate_f, rate_b, b_f, c_f, b_b, c_b)


def read_part(ref, index):
    state = ref[index, 0:N, :].astype(F32)
    tail = ref[index, N:ROWS, :].astype(F32)
    return state, tail[0:1] + tail[1:2] + tail[2:3]


def owned_decays(first, logs_ref, keep_ref):
    lane = lax.broadcasted_iota(jnp.int32, logs_ref.shape, 1)
    logs = logs_ref[...]
    low = jnp.sum(jnp.where(lane == first, logs, 0.0), axis=1, keepdims=True)
    high = jnp.sum(jnp.where(lane == first + 1, logs, 0.0), axis=1, keepdims=True)
    keep_ref[...] = jnp.exp(-jnp.where(lane < HEAD, low, high))


def decay_of(index, place_ref, keep_ref):
    along_y = (place_ref[3] - index // ZSIZE) & (YSIZE - 1)
    along_z = (place_ref[4] - index % ZSIZE) & (ZSIZE - 1)
    return keep_ref[pl.ds(along_z * YSIZE + along_y, 1), :]


def total_kernel(count, copies, place_ref, logs_ref, parts_ref, out_ref, keep_ref):
    backward = place_ref[0]
    owned_decays(place_ref[2], logs_ref, keep_ref)

    def step(i, carried):
        state, kept = carried
        index = jnp.where(backward == 1, count - 1 - i, i)
        keep = decay_of(index, place_ref, keep_ref)
        return keep * state + parts_ref[index].astype(F32), keep * kept

    state, kept = lax.fori_loop(
        0, count, step, (jnp.zeros((N, 128), F32), jnp.ones((1, 128), F32)), unroll=4
    )
    tail = three_rows(kept, 128)
    for g in range(copies):
        out_ref[g, 0:N, :] = state.astype(BF16)
        out_ref[g, N:ROWS, :] = tail


def entry_kernel(
    count, groups, place_ref, totals_ref, logs_ref, parts_ref, out_hbm, out_ref, keep_ref, sems
):
    backward, mine = place_ref[0], place_ref[1]
    owned_decays(place_ref[2], logs_ref, keep_ref)

    def outer(i, state):
        index = jnp.where(backward == 1, groups - 1 - i, i)
        own, keep = read_part(totals_ref, index)
        return keep * state + own

    state = lax.fori_loop(0, mine, outer, jnp.zeros((N, 128), F32))
    chunk = count // CHUNKS
    copies = []
    for q in range(CHUNKS):
        first = jnp.where(backward == 1, count - chunk * (q + 1), chunk * q)
        for i in range(chunk):
            index = first + jnp.where(backward == 1, chunk - 1 - i, i)
            out_ref[index] = state.astype(BF16)
            keep = decay_of(index, place_ref, keep_ref)
            state = keep * state + parts_ref[index].astype(F32)
        span = pl.ds(first, chunk)
        copies.append(pltpu.make_async_copy(out_ref.at[span], out_hbm.at[span], sems.at[q]))
        copies[-1].start()
    for copy in copies:
        copy.wait()


def vmem_specs(n):
    return [pl.BlockSpec(memory_space=pltpu.SMEM)] + [pl.BlockSpec(memory_space=pltpu.VMEM)] * n


def final_kernel(
    in_ref, silu_ref, scale_ref, m_ref, cf_ref, cb_ref, gain_ref, w_hbm,
    out_ref, normed_ref, w_ref, sems,
):
    copies = []
    for i in range(4):
        rows = pl.ds(E // 4 * i, E // 4)
        copies.append(pltpu.make_async_copy(w_hbm.at[rows], w_ref.at[rows], sems.at[i]))
        copies[-1].start()
    scales = [scale_ref[:, 2 * H * d : 2 * H * (d + 1)] for d in range(2)]
    square = jnp.zeros((Q, 128), F32)
    for j in range(E // FW):
        at = pl.ds(FW * j, FW)
        y = in_ref[:, at].astype(F32)
        select = head_select(j, 2 * H, FW, 0)
        for d, c_ref in enumerate((cf_ref, cb_ref)):
            m = jnp.concatenate([m_ref[d, FW // 128 * j + k] for k in range(FW // 128)], axis=1)
            y = y + dot(scales[d], select) * dot(c_ref[...], m)
        gated = y * silu_ref[:, at].astype(F32)
        for k in range(FW // 128):
            part = gated[:, 128 * k : 128 * (k + 1)]
            square = square + part * part
        normed_ref[:, at] = (gated * gain_ref[:, at]).astype(BF16)
    mean = jnp.sum(square, axis=1, keepdims=True) * (1.0 / E)
    scale = lax.rsqrt(mean + 1e-05)
    for copy in copies:
        copy.wait()
    for n in range(D // 256):
        at = pl.ds(256 * n, 256)
        out_ref[:, at] = (dot(normed_ref[...], w_ref[:, at]) * scale).astype(BF16)


def final_call(inside, silu, scale, m, c_f, c_b, gain, weight):
    return pl.pallas_call(
        final_kernel,
        in_specs=[pl.BlockSpec(memory_space=pltpu.VMEM)] * 7
        + [pl.BlockSpec(memory_space=pltpu.HBM)],
        out_specs=pl.BlockSpec(memory_space=pltpu.VMEM),
        out_shape=jax.ShapeDtypeStruct((Q, D), BF16),
        scratch_shapes=[
            pltpu.VMEM((Q, E), BF16),
            pltpu.VMEM((E, D), BF16),
            pltpu.SemaphoreType.DMA((4,)),
        ],
        compiler_params=pltpu.CompilerParams(vmem_limit_bytes=FINAL_VMEM),
        name="gate_norm_project",
    )(inside, silu, scale, m, c_f, c_b, gain, weight)


def per_device(
    features, gate_input, b_forward, c_forward, b_backward, c_backward,
    rate_forward, rate_backward, norm_gain, out_weight,
):
    count, groups = lax.axis_size("seq"), lax.axis_size("grp")
    states, logs = state_call(features, rate_forward, rate_backward, b_forward, b_backward)
    states = states.reshape(count, N, 128)
    member, group = lax.axis_index("seq"), lax.axis_index("grp")
    backward = (member >= count // 2).astype(jnp.int32)
    mine = jnp.where(backward == 1, groups - 1 - group, group)
    place = [backward, mine, 2 * member, member // ZSIZE, member % ZSIZE]
    place = jnp.stack(place).astype(jnp.int32)
    parts = lax.all_to_all(states, "seq", 0, 0, tiled=True)
    rows = [logs]
    for far in range(1, YSIZE):
        pairs = [(i, (i + far * ZSIZE) % count) for i in range(count)]
        rows.append(lax.ppermute(logs, "seq", pairs))
    logs = jnp.concatenate(rows, axis=0)
    rows = [logs]
    for far in range(1, ZSIZE):
        pairs = [(i, i // ZSIZE * ZSIZE + (i + far) % ZSIZE) for i in range(count)]
        rows.append(lax.ppermute(logs, "seq", pairs))
    logs = jnp.concatenate(rows, axis=0)
    keep = pltpu.VMEM((count, 128), F32)
    totals = pl.pallas_call(
        functools.partial(total_kernel, count, groups),
        in_specs=vmem_specs(2),
        out_specs=pl.BlockSpec(memory_space=pltpu.VMEM),
        out_shape=jax.ShapeDtypeStruct((groups, ROWS, 128), BF16),
        scratch_shapes=[keep],
        compiler_params=LIMIT,
        name="group_totals",
    )(place, logs, parts)
    totals = lax.all_to_all(totals, "grp", 0, 0, tiled=True)
    entries = pl.pallas_call(
        functools.partial(entry_kernel, count, groups),
        in_specs=vmem_specs(3),
        out_specs=pl.BlockSpec(memory_space=pltpu.HBM),
        out_shape=jax.ShapeDtypeStruct((count, N, 128), BF16),
        scratch_shapes=[
            pltpu.VMEM((count, N, 128), BF16),
            keep,
            pltpu.SemaphoreType.DMA((CHUNKS,)),
        ],
        compiler_params=LIMIT,
        name="entry_states",
    )(place, totals, logs, parts)
    m = lax.all_to_all(entries, "seq", 0, 0, tiled=True).reshape(2, E // 128, N, 128)
    inside, silu, scale = inside_call(
        features, gate_input, rate_forward, rate_backward,
        b_forward, c_forward, b_backward, c_backward,
    )
    return final_call(
        inside, silu, scale, m, c_forward, c_backward, norm_gain.reshape(1, E), out_weight
    )


def solution(mesh):
    rows = P(("grp", "seq"), None)
    heads = P(None, ("grp", "seq"))
    placed = (rows,) * 6 + (heads, heads, P(), P())
    return jax.shard_map(per_device, mesh=mesh, in_specs=placed, out_specs=rows, check_vma=False)
```

```python
import functools
import jax
import jax.numpy as jnp
from jax import lax
from jax.experimental import pallas as pl
from jax.experimental.pallas import tpu as pltpu
from jax.sharding import PartitionSpec as P

Q = 256
H = 32
HEAD = 64
N = 128
E = 2048
D = 1024
BLK = 256
STEPS = E // BLK
FW = 256
FINAL_VMEM = 48 * 1024 * 1024
HPB = BLK // HEAD
ROWS = N + 16
SHARE = N // 2
HALF = E // 2
PART = SHARE + 16
LOG2E = 1.4426950408889634
F32 = jnp.float32
BF16 = jnp.bfloat16
LIMIT = pltpu.CompilerParams(vmem_limit_bytes=24 * 1024 * 1024)


def lane_sums(r):
    width = r.shape[1]
    lane = lax.broadcasted_iota(jnp.int32, r.shape, 1)
    shift = 1
    while shift < width:
        r = r + jnp.where(lane >= shift, pltpu.roll(r, shift, 1), 0.0)
        shift *= 2
    return r


def lane_sums_back(r):
    width = r.shape[1]
    lane = lax.broadcasted_iota(jnp.int32, r.shape, 1)
    shift = 1
    while shift < width:
        r = r + jnp.where(lane < width - shift, pltpu.roll(r, width - shift, 1), 0.0)
        shift *= 2
    return r


def step_of(r):
    y = 2.0 * r
    s = jnp.full_like(y, 1.0)
    for k in range(9, 1, -1):
        s = 1.0 - y * (1.0 / k) * s
    return jnp.sqrt(jnp.where(y < 0.5, y * s, 1.0 - jnp.exp(-y)))


def two_parts(a):
    high = a.astype(BF16).astype(F32)
    return high, a - high


def head_select(block, rows, width, first):
    row = lax.broadcasted_iota(jnp.int32, (rows, width), 0) - first
    column = lax.broadcasted_iota(jnp.int32, (rows, width), 1)
    head = block * (width // HEAD) + column // HEAD
    return jnp.where((row == head) | (row == head + H), 1.0, 0.0).astype(BF16)


def dot(a, b):
    return jnp.dot(a, b, preferred_element_type=F32)


def tail_rows(values, width):
    row = lax.broadcasted_iota(jnp.int32, (16, width), 0)
    tail = jnp.zeros((16, width), F32)
    for i, value in enumerate(values):
        high, rest = two_parts(value)
        middle, low = two_parts(rest)
        for k, part in enumerate((high, middle, low)):
            tail = jnp.where(row == 3 * i + k, part, tail)
    return tail.astype(BF16)


def state_kernel(
    x_hbm, rf_hbm, rb_hbm, bf_hbm, bb_hbm, out_hbm,
    x_ref, r_ref, b_ref, select_ref, out_ref, sems,
):
    copies = [
        pltpu.make_async_copy(rf_hbm, r_ref.at[0], sems.at[0]),
        pltpu.make_async_copy(rb_hbm, r_ref.at[1], sems.at[1]),
        pltpu.make_async_copy(bf_hbm, b_ref.at[0], sems.at[2]),
        pltpu.make_async_copy(bb_hbm, b_ref.at[1], sems.at[3]),
        pltpu.make_async_copy(x_hbm, x_ref, sems.at[4]),
    ]
    for copy in copies:
        copy.start()
    select_ref[...] = head_select(0, 2 * H, E, 0)
    copies[0].wait()
    copies[1].wait()
    scales, keeps = [], []
    lane = lax.broadcasted_iota(jnp.int32, (H, 128), 1)
    for d, sums in enumerate((lane_sums, lane_sums_back)):
        r = r_ref[d]
        c = sums(r)
        total = c[:, Q - 1 : Q] if d == 0 else c[:, 0:1]
        parts = two_parts(step_of(r) * jnp.exp(c - total))
        scales.append(jnp.concatenate(parts, axis=0).T.astype(BF16))
        keeps.append(jnp.broadcast_to(jnp.exp(-total), (H, 128)))
    for k in range(E // 128):
        own = [
            jnp.where(lane[:1] < HEAD, keep[2 * k : 2 * k + 1], keep[2 * k + 1 : 2 * k + 2])
            for keep in keeps
        ]
        tail = tail_rows(own, 128)
        out_ref[2 * k, N:ROWS, :] = tail
        out_ref[2 * k + 1, N:ROWS, :] = tail
    copies[2].wait()
    copies[3].wait()
    turned = [b_ref[d].astype(F32).T.astype(BF16) for d in range(2)]
    copies[4].wait()
    for part in range(2):
        x = x_ref[:, HALF * part : HALF * (part + 1)].astype(F32)
        for d in range(2):
            factor = dot(scales[d], select_ref[:, HALF * part : HALF * (part + 1)])
            s = dot(turned[d], (x * factor).astype(BF16)).astype(BF16)
            for k in range(HALF // 128):
                for n in range(2):
                    out_ref[HALF // 64 * part + 2 * k + n, SHARE * d : SHARE * (d + 1), :] = s[
                        SHARE * n : SHARE * (n + 1), 128 * k : 128 * (k + 1)
                    ]
        span = pl.ds(HALF // 64 * part, HALF // 64)
        copies.append(pltpu.make_async_copy(out_ref.at[span], out_hbm.at[span], sems.at[5 + part]))
        copies[-1].start()
    copies[5].wait()
    copies[6].wait()


def state_call(x, rate_f, rate_b, b_f, b_b):
    return pl.pallas_call(
        state_kernel,
        in_specs=[pl.BlockSpec(memory_space=pltpu.HBM)] * 5,
        out_specs=pl.BlockSpec(memory_space=pltpu.HBM),
        out_shape=jax.ShapeDtypeStruct((2 * E // 128, ROWS, 128), BF16),
        scratch_shapes=[
            pltpu.VMEM((Q, E), BF16),
            pltpu.VMEM((2, H, Q), F32),
            pltpu.VMEM((2, Q, N), BF16),
            pltpu.VMEM((2 * H, E), BF16),
            pltpu.VMEM((2 * E // 128, ROWS, 128), BF16),
            pltpu.SemaphoreType.DMA((7,)),
        ],
        compiler_params=pltpu.CompilerParams(vmem_limit_bytes=60 * 1024 * 1024),
        name="span_states",
    )(x, rate_f, rate_b, b_f, b_b)


def inside_kernel(
    x_ref, gate_ref, rf_ref, rb_ref, bf_ref, cf_ref, bb_ref, cb_ref,
    out_ref, silu_ref, scale_ref, score_ref, rows_ref, cols_ref,
):
    j = pl.program_id(0)
    t = lax.broadcasted_iota(jnp.int32, (Q, Q), 0)
    s = lax.broadcasted_iota(jnp.int32, (Q, Q), 1)

    @pl.when(j == 0)
    def _():
        contract = (((1,), (1,)), ((), ()))
        forward = lax.dot_general(cf_ref[...], bf_ref[...], contract, preferred_element_type=F32)
        backward = lax.dot_general(cb_ref[...], bb_ref[...], contract, preferred_element_type=F32)
        score_ref[...] = jnp.where(s <= t, forward, backward)
        own = jnp.sum(jnp.where(s == t, backward, 0.0), axis=0, keepdims=True)
        c_f = lane_sums(rf_ref[...]) * LOG2E
        c_b = lane_sums_back(rb_ref[...]) * LOG2E
        step_f = step_of(rf_ref[...])
        step_b = step_of(rb_ref[...])
        rows_ref[0] = c_f + jnp.log(step_f) * LOG2E
        rows_ref[1] = c_b + jnp.log(step_b) * LOG2E
        high, low = two_parts(own * step_b)
        cols_ref[...] = jnp.concatenate([c_f, c_b, high, low], axis=0).T
        parts = two_parts(jnp.exp2(-c_f)) + two_parts(jnp.exp2(-c_b))
        scale_ref[...] = jnp.concatenate(parts, axis=0).T.astype(BF16)

    gate = gate_ref[...].astype(F32)
    silu_ref[...] = (gate * jax.nn.sigmoid(gate)).astype(BF16)
    cols = cols_ref[...]
    own = dot(cols.astype(BF16), head_select(j, 4 * H, BLK, 2 * H))
    cols = pltpu.roll(cols, lax.rem(4 * H - HPB * j, 4 * H), 1)
    lane = lax.broadcasted_iota(jnp.int32, (Q, 128), 1)
    for p in range(HPB // 2):
        x = x_ref[:, 128 * p : 128 * (p + 1)]
        halves = []
        for i in (2 * p, 2 * p + 1):
            forward = rows_ref[0, pl.ds(HPB * j + i, 1), :] - cols[:, i : i + 1]
            backward = rows_ref[1, pl.ds(HPB * j + i, 1), :] - cols[:, H + i : H + i + 1]
            w = score_ref[...] * jnp.exp2(jnp.where(s <= t, forward, backward))
            halves.append(dot(w.astype(BF16), x))
        y = jnp.where(lane < HEAD, halves[0], halves[1])
        y = y + own[:, 128 * p : 128 * (p + 1)] * x.astype(F32)
        out_ref[:, 128 * p : 128 * (p + 1)] = y.astype(BF16)


def inside_call(x, gate, rate_f, rate_b, b_f, c_f, b_b, c_b):
    whole = lambda shape: pl.BlockSpec(shape, lambda j: (0,) * len(shape))
    columns = pl.BlockSpec((Q, BLK), lambda j: (0, j))
    return pl.pallas_call(
        inside_kernel,
        grid=(STEPS,),
        in_specs=[columns, columns, whole((H, Q)), whole((H, Q))] + [whole((Q, N))] * 4,
        out_specs=[columns, columns, whole((Q, 4 * H))],
        out_shape=[jax.ShapeDtypeStruct((Q, E), BF16)] * 2
        + [jax.ShapeDtypeStruct((Q, 4 * H), BF16)],
        compiler_params=LIMIT,
        scratch_shapes=[
            pltpu.VMEM((Q, Q), F32),
            pltpu.VMEM((2, H, Q), F32),
            pltpu.VMEM((Q, 4 * H), F32),
        ],
        cost_estimate=pl.CostEstimate(
            flops=2 * H * Q * Q * 128, bytes_accessed=4 * Q * E * 2, transcendentals=H * Q * Q
        ),
        name="inside_spans",
    )(x, gate, rate_f, rate_b, b_f, c_f, b_b, c_b)


def read_part(ref, index, d):
    state = ref[index, SHARE * d : SHARE * (d + 1), :].astype(F32)
    tail = ref[index, N:ROWS, :].astype(F32)
    return state, tail[3 * d : 3 * d + 1] + tail[3 * d + 1 : 3 * d + 2] + tail[3 * d + 2 : 3 * d + 3]


def total_kernel(count, groups, group_ref, parts_ref, out_ref):
    def step(i, carried):
        result = []
        for d in range(2):
            state, kept = carried[2 * d : 2 * d + 2]
            own, keep = read_part(parts_ref, i if d == 0 else count - 1 - i, d)
            result += [keep * state + own, keep * kept]
        return tuple(result)

    start = (jnp.zeros((SHARE, 128), F32), jnp.ones((1, 128), F32))
    result = lax.fori_loop(0, count, step, start + start, unroll=4)
    states = [result[2 * d].astype(BF16) for d in range(2)]
    tails = [tail_rows([result[2 * d + 1]], 128) for d in range(2)]
    for g in range(groups):
        later = g > group_ref[0]

        @pl.when(later)
        def _():
            out_ref[g, 0:SHARE, :] = states[0]
            out_ref[g, SHARE:PART, :] = tails[0]

        @pl.when(jnp.logical_not(later))
        def _():
            out_ref[g, 0:SHARE, :] = states[1]
            out_ref[g, SHARE:PART, :] = tails[1]


def entry_kernel(count, groups, group_ref, totals_ref, parts_ref, out_hbm, out_ref, sems):
    group = group_ref[0]

    def outer(index, state):
        own = totals_ref[index, 0:SHARE, :].astype(F32)
        tail = totals_ref[index, SHARE:PART, :].astype(F32)
        return (tail[0:1] + tail[1:2] + tail[2:3]) * state + own

    empty = jnp.zeros((SHARE, 128), F32)
    forward = lax.fori_loop(0, group, outer, empty)
    backward = lax.fori_loop(
        0, groups - 1 - group, lambda i, state: outer(groups - 1 - i, state), empty
    )
    states = [forward, backward]
    for i in range(count):
        for d in range(2):
            index = i if d == 0 else count - 1 - i
            out_ref[index, SHARE * d : SHARE * (d + 1), :] = states[d].astype(BF16)
            own, keep = read_part(parts_ref, index, d)
            states[d] = keep * states[d] + own
    copy = pltpu.make_async_copy(out_ref, out_hbm, sems.at[0])
    copy.start()
    copy.wait()


def vmem_specs(n):
    return [pl.BlockSpec(memory_space=pltpu.SMEM)] + [pl.BlockSpec(memory_space=pltpu.VMEM)] * n


def state_of(ref, d, block):
    rows = pl.ds(SHARE * d, SHARE)
    return jnp.concatenate([ref[2 * block, rows, :], ref[2 * block + 1, rows, :]], axis=0)


def final_kernel(
    in_ref, silu_ref, scale_ref, m_ref, cf_ref, cb_ref, gain_ref, w_hbm,
    out_ref, normed_ref, w_ref, sems,
):
    copies = []
    for i in range(4):
        rows = pl.ds(E // 4 * i, E // 4)
        copies.append(pltpu.make_async_copy(w_hbm.at[rows], w_ref.at[rows], sems.at[i]))
        copies[-1].start()
    scales = [scale_ref[:, 2 * H * d : 2 * H * (d + 1)] for d in range(2)]
    square = jnp.zeros((Q, 128), F32)
    for j in range(E // FW):
        at = pl.ds(FW * j, FW)
        y = in_ref[:, at].astype(F32)
        select = head_select(j, 2 * H, FW, 0)
        for d, c_ref in enumerate((cf_ref, cb_ref)):
            m = jnp.concatenate([state_of(m_ref, d, FW // 128 * j + k) for k in range(FW // 128)], 1)
            y = y + dot(scales[d], select) * dot(c_ref[...], m)
        gated = y * silu_ref[:, at].astype(F32)
        for k in range(FW // 128):
            part = gated[:, 128 * k : 128 * (k + 1)]
            square = square + part * part
        normed_ref[:, at] = (gated * gain_ref[:, at]).astype(BF16)
    mean = jnp.sum(square, axis=1, keepdims=True) * (1.0 / E)
    scale = lax.rsqrt(mean + 1e-05)
    for copy in copies:
        copy.wait()
    for n in range(D // 256):
        at = pl.ds(256 * n, 256)
        out_ref[:, at] = (dot(normed_ref[...], w_ref[:, at]) * scale).astype(BF16)


def final_call(inside, silu, scale, m, c_f, c_b, gain, weight):
    return pl.pallas_call(
        final_kernel,
        in_specs=[pl.BlockSpec(memory_space=pltpu.VMEM)] * 7
        + [pl.BlockSpec(memory_space=pltpu.HBM)],
        out_specs=pl.BlockSpec(memory_space=pltpu.VMEM),
        out_shape=jax.ShapeDtypeStruct((Q, D), BF16),
        scratch_shapes=[
            pltpu.VMEM((Q, E), BF16),
            pltpu.VMEM((E, D), BF16),
            pltpu.SemaphoreType.DMA((4,)),
        ],
        compiler_params=pltpu.CompilerParams(vmem_limit_bytes=FINAL_VMEM),
        name="gate_norm_project",
    )(inside, silu, scale, m, c_f, c_b, gain, weight)


def per_device(
    features, gate_input, b_forward, c_forward, b_backward, c_backward,
    rate_forward, rate_backward, norm_gain, out_weight,
):
    count, groups = lax.axis_size("seq"), lax.axis_size("grp")
    states = state_call(features, rate_forward, rate_backward, b_forward, b_backward)
    place = lax.axis_index("grp").astype(jnp.int32).reshape(1)
    parts = lax.all_to_all(states, "seq", 0, 0, tiled=True)
    totals = pl.pallas_call(
        functools.partial(total_kernel, count, groups),
        in_specs=vmem_specs(1),
        out_specs=pl.BlockSpec(memory_space=pltpu.VMEM),
        out_shape=jax.ShapeDtypeStruct((groups, PART, 128), BF16),
        compiler_params=LIMIT,
        name="group_totals",
    )(place, parts)
    totals = lax.all_to_all(totals, "grp", 0, 0, tiled=True)
    entries = pl.pallas_call(
        functools.partial(entry_kernel, count, groups),
        in_specs=vmem_specs(2),
        out_specs=pl.BlockSpec(memory_space=pltpu.HBM),
        out_shape=jax.ShapeDtypeStruct((count, N, 128), BF16),
        scratch_shapes=[
            pltpu.VMEM((count, N, 128), BF16),
            pltpu.SemaphoreType.DMA((1,)),
        ],
        compiler_params=LIMIT,
        name="entry_states",
    )(place, totals, parts)
    m = lax.all_to_all(entries, "seq", 0, 0, tiled=True)
    inside, silu, scale = inside_call(
        features, gate_input, rate_forward, rate_backward,
        b_forward, c_forward, b_backward, c_backward,
    )
    return final_call(
        inside, silu, scale, m, c_forward, c_backward, norm_gain.reshape(1, E), out_weight
    )


def solution(mesh):
    rows = P(("grp", "seq"), None)
    heads = P(None, ("grp", "seq"))
    placed = (rows,) * 6 + (heads, heads, P(), P())
    return jax.shard_map(per_device, mesh=mesh, in_specs=placed, out_specs=rows, check_vma=False)
```

```python
import functools
import jax
import jax.numpy as jnp
from jax import lax
from jax.experimental import pallas as pl
from jax.experimental.pallas import tpu as pltpu
from jax.sharding import PartitionSpec as P

Q = 256
H = 32
HEAD = 64
N = 128
E = 2048
D = 1024
BLK = 256
STEPS = E // BLK
FW = 256
FINAL_VMEM = 48 * 1024 * 1024
HPB = BLK // HEAD
ROWS = N + 16
SHARE = N // 2
HALF = E // 2
PART = SHARE + 16
LOG2E = 1.4426950408889634
F32 = jnp.float32
BF16 = jnp.bfloat16
LIMIT = pltpu.CompilerParams(vmem_limit_bytes=24 * 1024 * 1024)


def lane_sums(r):
    width = r.shape[1]
    lane = lax.broadcasted_iota(jnp.int32, r.shape, 1)
    shift = 1
    while shift < width:
        r = r + jnp.where(lane >= shift, pltpu.roll(r, shift, 1), 0.0)
        shift *= 2
    return r


def lane_sums_back(r):
    width = r.shape[1]
    lane = lax.broadcasted_iota(jnp.int32, r.shape, 1)
    shift = 1
    while shift < width:
        r = r + jnp.where(lane < width - shift, pltpu.roll(r, width - shift, 1), 0.0)
        shift *= 2
    return r


def step_of(r):
    y = 2.0 * r
    s = jnp.full_like(y, 1.0)
    for k in range(9, 1, -1):
        s = 1.0 - y * (1.0 / k) * s
    return jnp.sqrt(jnp.where(y < 0.5, y * s, 1.0 - jnp.exp(-y)))


def two_parts(a):
    high = a.astype(BF16).astype(F32)
    return high, a - high


def head_select(block, rows, width, first):
    row = lax.broadcasted_iota(jnp.int32, (rows, width), 0) - first
    column = lax.broadcasted_iota(jnp.int32, (rows, width), 1)
    head = block * (width // HEAD) + column // HEAD
    return jnp.where((row == head) | (row == head + H), 1.0, 0.0).astype(BF16)


def dot(a, b):
    return jnp.dot(a, b, preferred_element_type=F32)


def tail_rows(values, width):
    row = lax.broadcasted_iota(jnp.int32, (16, width), 0)
    tail = jnp.zeros((16, width), F32)
    for i, value in enumerate(values):
        high, rest = two_parts(value)
        middle, low = two_parts(rest)
        for k, part in enumerate((high, middle, low)):
            tail = jnp.where(row == 3 * i + k, part, tail)
    return tail.astype(BF16)


def state_kernel(
    x_hbm, rf_hbm, rb_hbm, bf_hbm, bb_hbm, out_hbm,
    x_ref, r_ref, b_ref, select_ref, out_ref, sems,
):
    copies = [
        pltpu.make_async_copy(rf_hbm, r_ref.at[0], sems.at[0]),
        pltpu.make_async_copy(rb_hbm, r_ref.at[1], sems.at[1]),
        pltpu.make_async_copy(bf_hbm, b_ref.at[0], sems.at[2]),
        pltpu.make_async_copy(bb_hbm, b_ref.at[1], sems.at[3]),
        pltpu.make_async_copy(x_hbm, x_ref, sems.at[4]),
    ]
    for copy in copies:
        copy.start()
    select_ref[...] = head_select(0, 2 * H, E, 0)
    copies[0].wait()
    copies[1].wait()
    scales, keeps = [], []
    lane = lax.broadcasted_iota(jnp.int32, (H, 128), 1)
    for d, sums in enumerate((lane_sums, lane_sums_back)):
        r = r_ref[d]
        c = sums(r)
        total = c[:, Q - 1 : Q] if d == 0 else c[:, 0:1]
        parts = two_parts(step_of(r) * jnp.exp(c - total))
        scales.append(jnp.concatenate(parts, axis=0).T.astype(BF16))
        keeps.append(jnp.broadcast_to(jnp.exp(-total), (H, 128)))
    for k in range(E // 128):
        own = [
            jnp.where(lane[:1] < HEAD, keep[2 * k : 2 * k + 1], keep[2 * k + 1 : 2 * k + 2])
            for keep in keeps
        ]
        tail = tail_rows(own, 128)
        out_ref[2 * k, N:ROWS, :] = tail
        out_ref[2 * k + 1, N:ROWS, :] = tail
    copies[2].wait()
    copies[3].wait()
    turned = [b_ref[d].astype(F32).T.astype(BF16) for d in range(2)]
    copies[4].wait()
    x = x_ref[...].astype(F32)
    scaled = [(x * dot(scales[d], select_ref[...])).astype(BF16) for d in range(2)]
    for part in range(2):
        for d in range(2):
            s = dot(turned[d], scaled[d][:, HALF * part : HALF * (part + 1)]).astype(BF16)
            for k in range(HALF // 128):
                for n in range(2):
                    out_ref[HALF // 64 * part + 2 * k + n, SHARE * d : SHARE * (d + 1), :] = s[
                        SHARE * n : SHARE * (n + 1), 128 * k : 128 * (k + 1)
                    ]
        span = pl.ds(HALF // 64 * part, HALF // 64)
        copies.append(pltpu.make_async_copy(out_ref.at[span], out_hbm.at[span], sems.at[5 + part]))
        copies[-1].start()
    copies[5].wait()
    copies[6].wait()


def state_call(x, rate_f, rate_b, b_f, b_b):
    return pl.pallas_call(
        state_kernel,
        in_specs=[pl.BlockSpec(memory_space=pltpu.HBM)] * 5,
        out_specs=pl.BlockSpec(memory_space=pltpu.HBM),
        out_shape=jax.ShapeDtypeStruct((2 * E // 128, ROWS, 128), BF16),
        scratch_shapes=[
            pltpu.VMEM((Q, E), BF16),
            pltpu.VMEM((2, H, Q), F32),
            pltpu.VMEM((2, Q, N), BF16),
            pltpu.VMEM((2 * H, E), BF16),
            pltpu.VMEM((2 * E // 128, ROWS, 128), BF16),
            pltpu.SemaphoreType.DMA((7,)),
        ],
        compiler_params=pltpu.CompilerParams(vmem_limit_bytes=60 * 1024 * 1024),
        name="span_states",
    )(x, rate_f, rate_b, b_f, b_b)


def inside_kernel(
    x_ref, gate_ref, rf_ref, rb_ref, bf_ref, cf_ref, bb_ref, cb_ref,
    out_ref, silu_ref, scale_ref, score_ref, rows_ref, cols_ref,
):
    j = pl.program_id(0)
    t = lax.broadcasted_iota(jnp.int32, (Q, Q), 0)
    s = lax.broadcasted_iota(jnp.int32, (Q, Q), 1)

    @pl.when(j == 0)
    def _():
        contract = (((1,), (1,)), ((), ()))
        forward = lax.dot_general(cf_ref[...], bf_ref[...], contract, preferred_element_type=F32)
        backward = lax.dot_general(cb_ref[...], bb_ref[...], contract, preferred_element_type=F32)
        score_ref[...] = jnp.where(s <= t, forward, backward)
        own = jnp.sum(jnp.where(s == t, backward, 0.0), axis=0, keepdims=True)
        c_f = lane_sums(rf_ref[...]) * LOG2E
        c_b = lane_sums_back(rb_ref[...]) * LOG2E
        step_f = step_of(rf_ref[...])
        step_b = step_of(rb_ref[...])
        rows_ref[0] = c_f + jnp.log(step_f) * LOG2E
        rows_ref[1] = c_b + jnp.log(step_b) * LOG2E
        high, low = two_parts(own * step_b)
        cols_ref[...] = jnp.concatenate([c_f, c_b, high, low], axis=0).T
        parts = two_parts(jnp.exp2(-c_f)) + two_parts(jnp.exp2(-c_b))
        scale_ref[...] = jnp.concatenate(parts, axis=0).T.astype(BF16)

    gate = gate_ref[...].astype(F32)
    silu_ref[...] = (gate * jax.nn.sigmoid(gate)).astype(BF16)
    cols = cols_ref[...]
    own = dot(cols.astype(BF16), head_select(j, 4 * H, BLK, 2 * H))
    cols = pltpu.roll(cols, lax.rem(4 * H - HPB * j, 4 * H), 1)
    lane = lax.broadcasted_iota(jnp.int32, (Q, 128), 1)
    for p in range(HPB // 2):
        x = x_ref[:, 128 * p : 128 * (p + 1)]
        halves = []
        for i in (2 * p, 2 * p + 1):
            forward = rows_ref[0, pl.ds(HPB * j + i, 1), :] - cols[:, i : i + 1]
            backward = rows_ref[1, pl.ds(HPB * j + i, 1), :] - cols[:, H + i : H + i + 1]
            w = score_ref[...] * jnp.exp2(jnp.where(s <= t, forward, backward))
            halves.append(dot(w.astype(BF16), x))
        y = jnp.where(lane < HEAD, halves[0], halves[1])
        y = y + own[:, 128 * p : 128 * (p + 1)] * x.astype(F32)
        out_ref[:, 128 * p : 128 * (p + 1)] = y.astype(BF16)


def inside_call(x, gate, rate_f, rate_b, b_f, c_f, b_b, c_b):
    whole = lambda shape: pl.BlockSpec(shape, lambda j: (0,) * len(shape))
    columns = pl.BlockSpec((Q, BLK), lambda j: (0, j))
    return pl.pallas_call(
        inside_kernel,
        grid=(STEPS,),
        in_specs=[columns, columns, whole((H, Q)), whole((H, Q))] + [whole((Q, N))] * 4,
        out_specs=[columns, columns, whole((Q, 4 * H))],
        out_shape=[jax.ShapeDtypeStruct((Q, E), BF16)] * 2
        + [jax.ShapeDtypeStruct((Q, 4 * H), BF16)],
        compiler_params=LIMIT,
        scratch_shapes=[
            pltpu.VMEM((Q, Q), F32),
            pltpu.VMEM((2, H, Q), F32),
            pltpu.VMEM((Q, 4 * H), F32),
        ],
        cost_estimate=pl.CostEstimate(
            flops=2 * H * Q * Q * 128, bytes_accessed=4 * Q * E * 2, transcendentals=H * Q * Q
        ),
        name="inside_spans",
    )(x, gate, rate_f, rate_b, b_f, c_f, b_b, c_b)


def read_part(ref, index, d):
    state = ref[index, SHARE * d : SHARE * (d + 1), :].astype(F32)
    tail = ref[index, N:ROWS, :].astype(F32)
    return state, tail[3 * d : 3 * d + 1] + tail[3 * d + 1 : 3 * d + 2] + tail[3 * d + 2 : 3 * d + 3]


def total_kernel(count, groups, group_ref, parts_ref, out_ref):
    def step(i, carried):
        result = []
        for d in range(2):
            state, kept = carried[2 * d : 2 * d + 2]
            own, keep = read_part(parts_ref, i if d == 0 else count - 1 - i, d)
            result += [keep * state + own, keep * kept]
        return tuple(result)

    start = (jnp.zeros((SHARE, 128), F32), jnp.ones((1, 128), F32))
    result = lax.fori_loop(0, count, step, start + start, unroll=4)
    states = [result[2 * d].astype(BF16) for d in range(2)]
    tails = [tail_rows([result[2 * d + 1]], 128) for d in range(2)]
    for g in range(groups):
        later = g > group_ref[0]

        @pl.when(later)
        def _():
            out_ref[g, 0:SHARE, :] = states[0]
            out_ref[g, SHARE:PART, :] = tails[0]

        @pl.when(jnp.logical_not(later))
        def _():
            out_ref[g, 0:SHARE, :] = states[1]
            out_ref[g, SHARE:PART, :] = tails[1]


def entry_kernel(count, groups, group_ref, totals_ref, parts_ref, out_hbm, out_ref, sems):
    group = group_ref[0]

    def outer(index, state):
        own = totals_ref[index, 0:SHARE, :].astype(F32)
        tail = totals_ref[index, SHARE:PART, :].astype(F32)
        return (tail[0:1] + tail[1:2] + tail[2:3]) * state + own

    empty = jnp.zeros((SHARE, 128), F32)
    forward = lax.fori_loop(0, group, outer, empty)
    backward = lax.fori_loop(
        0, groups - 1 - group, lambda i, state: outer(groups - 1 - i, state), empty
    )
    states = [forward, backward]
    for i in range(count):
        for d in range(2):
            index = i if d == 0 else count - 1 - i
            out_ref[index, SHARE * d : SHARE * (d + 1), :] = states[d].astype(BF16)
            own, keep = read_part(parts_ref, index, d)
            states[d] = keep * states[d] + own
    copy = pltpu.make_async_copy(out_ref, out_hbm, sems.at[0])
    copy.start()
    copy.wait()


def vmem_specs(n):
    return [pl.BlockSpec(memory_space=pltpu.SMEM)] + [pl.BlockSpec(memory_space=pltpu.VMEM)] * n


def state_of(ref, d, block):
    rows = pl.ds(SHARE * d, SHARE)
    return jnp.concatenate([ref[2 * block, rows, :], ref[2 * block + 1, rows, :]], axis=0)


def final_kernel(
    in_ref, silu_ref, scale_ref, m_ref, cf_ref, cb_ref, gain_ref, w_hbm,
    out_ref, normed_ref, w_ref, sems,
):
    copies = []
    for i in range(2):
        rows = pl.ds(E // 2 * i, E // 2)
        copies.append(pltpu.make_async_copy(w_hbm.at[rows], w_ref.at[rows], sems.at[i]))
        copies[-1].start()
    scales = [scale_ref[:, 2 * H * d : 2 * H * (d + 1)] for d in range(2)]
    square = jnp.zeros((Q, 128), F32)
    for j in range(E // FW):
        at = pl.ds(FW * j, FW)
        y = in_ref[:, at].astype(F32)
        select = head_select(j, 2 * H, FW, 0)
        for d, c_ref in enumerate((cf_ref, cb_ref)):
            m = jnp.concatenate([state_of(m_ref, d, FW // 128 * j + k) for k in range(FW // 128)], 1)
            y = y + dot(scales[d], select) * dot(c_ref[...], m)
        gated = y * silu_ref[:, at].astype(F32)
        for k in range(FW // 128):
            part = gated[:, 128 * k : 128 * (k + 1)]
            square = square + part * part
        normed_ref[:, at] = (gated * gain_ref[:, at]).astype(BF16)
    mean = jnp.sum(square, axis=1, keepdims=True) * (1.0 / E)
    scale = lax.rsqrt(mean + 1e-05)
    for copy in copies:
        copy.wait()
    for n in range(D // 256):
        at = pl.ds(256 * n, 256)
        out_ref[:, at] = (dot(normed_ref[...], w_ref[:, at]) * scale).astype(BF16)


def final_call(inside, silu, scale, m, c_f, c_b, gain, weight):
    return pl.pallas_call(
        final_kernel,
        in_specs=[pl.BlockSpec(memory_space=pltpu.VMEM)] * 7
        + [pl.BlockSpec(memory_space=pltpu.HBM)],
        out_specs=pl.BlockSpec(memory_space=pltpu.VMEM),
        out_shape=jax.ShapeDtypeStruct((Q, D), BF16),
        scratch_shapes=[
            pltpu.VMEM((Q, E), BF16),
            pltpu.VMEM((E, D), BF16),
            pltpu.SemaphoreType.DMA((2,)),
        ],
        compiler_params=pltpu.CompilerParams(vmem_limit_bytes=FINAL_VMEM),
        name="gate_norm_project",
    )(inside, silu, scale, m, c_f, c_b, gain, weight)


def per_device(
    features, gate_input, b_forward, c_forward, b_backward, c_backward,
    rate_forward, rate_backward, norm_gain, out_weight,
):
    count, groups = lax.axis_size("seq"), lax.axis_size("grp")
    states = state_call(features, rate_forward, rate_backward, b_forward, b_backward)
    place = lax.axis_index("grp").astype(jnp.int32).reshape(1)
    parts = lax.all_to_all(states, "seq", 0, 0, tiled=True)
    totals = pl.pallas_call(
        functools.partial(total_kernel, count, groups),
        in_specs=vmem_specs(1),
        out_specs=pl.BlockSpec(memory_space=pltpu.VMEM),
        out_shape=jax.ShapeDtypeStruct((groups, PART, 128), BF16),
        compiler_params=LIMIT,
        name="group_totals",
    )(place, parts)
    totals = lax.all_to_all(totals, "grp", 0, 0, tiled=True)
    entries = pl.pallas_call(
        functools.partial(entry_kernel, count, groups),
        in_specs=vmem_specs(2),
        out_specs=pl.BlockSpec(memory_space=pltpu.HBM),
        out_shape=jax.ShapeDtypeStruct((count, N, 128), BF16),
        scratch_shapes=[
            pltpu.VMEM((count, N, 128), BF16),
            pltpu.SemaphoreType.DMA((1,)),
        ],
        compiler_params=LIMIT,
        name="entry_states",
    )(place, totals, parts)
    m = lax.all_to_all(entries, "seq", 0, 0, tiled=True)
    inside, silu, scale = inside_call(
        features, gate_input, rate_forward, rate_backward,
        b_forward, c_forward, b_backward, c_backward,
    )
    return final_call(
        inside, silu, scale, m, c_forward, c_backward, norm_gain.reshape(1, E), out_weight
    )


def solution(mesh):
    rows = P(("grp", "seq"), None)
    heads = P(None, ("grp", "seq"))
    placed = (rows,) * 6 + (heads, heads, P(), P())
    return jax.shard_map(per_device, mesh=mesh, in_specs=placed, out_specs=rows, check_vma=False)
```
